32 devices in a mesh: groups: 2 (over y), dp: 4 (over z), tgt: 4 (over x, core).
Axes of the slice: x: 2, y: 2, z: 4, core: 2. Of those that a mesh axis runs over, the one named last changes fastest.
Arguments:
- hidden: bfloat16 [6144, 4096], P(('groups', 'dp', 'tgt')), parts along dimension 0, may hold values from -6 to 6
- cotangent: bfloat16 [6144, 4096], P(('groups', 'dp', 'tgt')), parts along dimension 0, may hold values from -6 to 6
- adapter_down_weight: bfloat16 [4096, 64], replicated, may hold values from -0.09375 to 0.09375
- adapter_up_weight: bfloat16 [64, 4096], replicated, may hold values from -0.75 to 0.75
- width_projection_factor: bfloat16 [4096, 512], replicated, may hold values from -0.09375 to 0.09375
- rank_projection_factor: bfloat16 [64, 8], replicated, may hold values from -0.75 to 0.75
- targets: bfloat16 [8, 768, 8192], P(('groups', 'dp'), 'tgt'), parts along dimension 0, may hold values from -100 to 100
- strata: int32 [768], P(('groups', 'dp', 'tgt')), parts along dimension 0, may hold values from 0 to 31
- keep: int32 [768], P(('groups', 'dp', 'tgt')), parts along dimension 0, may hold values from 0 to 1
- shard_example_count: int32 [32], P(('groups', 'dp', 'tgt')), parts along dimension 0, may hold values from 18 to 24
- stratum_owner_table: int32 [32], replicated, may hold values from 0 to 3, as said below
Outputs:
- selection: float32 [768], P(('groups', 'dp', 'tgt')), parts along dimension 0
The draws below stay inside these ranges and needn't reach their ends.
There are 2 independent parts, one for each index of `groups`. The reference program is written for one: setup_inputs(seed, part) draws one part's arguments, and reference() takes and returns one part's arrays. A program takes and returns all parts, laid end to end along the dimension named above; an argument that names none is the same for every part. Nothing has to cross between parts.
Inputs may be any that keep to these rules, and one draw needn't show every extreme that they name: `stratum_owner_table`: each of the 4 owners holds exactly 8 strata.
All inputs are finite; a program needn't handle non-finite values.
Results may differ from the reference program's by a relative error of at most 0.0029.
Values may be sent and summed in bfloat16 or wider, within the bound.
No kernel may reach another device: no remote copies, remote signals or barrier semaphores. Data moves between devices by JAX's collectives and lax.ppermute only.
A program may use at most 64 MiB of HBM per device.

```python
import math
import jax
import jax.numpy as jnp
import numpy as np
from jax import lax

MODEL_WIDTH = 4096
ADAPTER_RANK = 64
KD = 512
KR = 8
FEAT = 8192
SEQ = 8
EX_DEV = 24
CAP = 2
TGT = 768
TASKS = 16
OWNERS = 4
NSTRATA = 32
SHARDS = 16
EXAMPLES = 384
TOKENS = 3072


def draw_keep(key, part):
    position = jnp.arange(EXAMPLES, dtype=jnp.int32)
    threshold = 330 + 670 * position // EXAMPLES
    ticket = jax.random.randint(key, (EXAMPLES,), 0, 1000, dtype=jnp.int32)
    return (ticket < threshold).astype(jnp.int32)


def draw_shard_example_count(key, part):
    drawn_counts = jax.random.randint(key, (SHARDS,), max(1, 3 * EX_DEV // 4), EX_DEV + 1, dtype=jnp.int32)
    chosen = jax.random.randint(jax.random.fold_in(key, 7), (), 0, SHARDS, dtype=jnp.int32)
    return jnp.where(jnp.arange(SHARDS, dtype=jnp.int32) == chosen, EX_DEV, drawn_counts).astype(jnp.int32)


def draw_stratum_owner_table(key, part):
    shuffled = jax.random.permutation(key, NSTRATA).astype(jnp.int32)
    return (shuffled % OWNERS).astype(jnp.int32)


def draw_targets(key, part):
    per_task = TGT // TASKS
    centers = jax.random.normal(jax.random.fold_in(key, 1), (OWNERS, TASKS, 1, FEAT), jnp.float32)
    target_noise = jax.random.normal(jax.random.fold_in(key, 2), (OWNERS, TASKS, per_task, FEAT), jnp.float32)
    values = centers + target_noise
    return values.reshape(OWNERS, TGT, FEAT).astype(jnp.bfloat16)


def with_ends(values, own_key, least, largest):
    spot = [jax.random.randint(jax.random.fold_in(own_key, axis), (), 0, length) for axis, length in enumerate(values.shape)]
    widest = values.shape.index(max(values.shape))
    neighbour = spot[:widest] + [(spot[widest] + 1) % values.shape[widest]] + spot[widest + 1:]
    return values.at[tuple(spot)].set(least).at[tuple(neighbour)].set(largest)


def steps_of(rng, dims, cuts, low, top_value):
    def one(axis_at, parts):
        heights = jax.random.uniform(jax.random.fold_in(jax.random.fold_in(rng, 6), axis_at), (parts,), jnp.float32, low / len(cuts), top_value / len(cuts))
        return jnp.repeat(jnp.exp(heights), dims[axis_at] // parts).reshape((-1,) + (1,) * (len(dims) - axis_at - 1))

    loudness = one(*cuts[0])
    for cut in cuts[1:]:
        loudness = loudness * one(*cut)
    return loudness


def rank_bounds(amount, slope):
    loads = [(1 << 20) // math.isqrt(standing ** slope) + 1 for standing in range(1, amount + 1)]
    scale = 1 + sum(loads) // (1 << 30)
    return np.cumsum(np.array([max(1, weight // scale) for weight in loads]))


def ranked(own_key, dims, number_of, lean):
    grid = rank_bounds(number_of, lean)
    lot = jax.random.randint(jax.random.fold_in(own_key, 1), dims, 0, int(grid[number_of - 1]))
    rank = jnp.searchsorted(jnp.asarray(grid, jnp.int32), lot, side="right")
    return jax.random.permutation(jax.random.fold_in(own_key, 2), number_of)[rank].astype(jnp.int32)


def bell_draw(stream_key, dims, scale, reach, pieces=(), kind=jnp.bfloat16):
    values = jax.random.normal(stream_key, dims, jnp.float32) * scale
    if len(pieces) > 0:
        values = steps_of(stream_key, dims, pieces, -0.22, 0.18) * values
    return jnp.clip(values, min=-reach, max=reach).astype(kind)


def setup_inputs(seed: int = 0, part: int = 0) -> dict:
    splits = jax.random.split(jax.random.key(seed), 12)
    own_keys = jax.random.split(jax.random.fold_in(splits[11], part), 12)
    hidden = bell_draw(own_keys[0], (TOKENS, MODEL_WIDTH), 1.0, 6.0, ((0, 16),))
    cotangent = bell_draw(own_keys[1], (TOKENS, MODEL_WIDTH), 1.0, 6.0, ((0, 16),))
    adapter_down_weight = bell_draw(splits[2], (MODEL_WIDTH, ADAPTER_RANK), MODEL_WIDTH ** -0.5, 0.09375)
    adapter_up_weight = bell_draw(splits[3], (ADAPTER_RANK, MODEL_WIDTH), ADAPTER_RANK ** -0.5, 0.75)
    width_projection_factor = bell_draw(splits[4], (MODEL_WIDTH, KD), MODEL_WIDTH ** -0.5, 0.09375)
    rank_projection_factor = bell_draw(splits[5], (ADAPTER_RANK, KR), ADAPTER_RANK ** -0.5, 0.75)
    targets = draw_targets(jax.random.fold_in(jax.random.fold_in(splits[11], part), 71), part)
    strata = with_ends(ranked(own_keys[7], (EXAMPLES,), NSTRATA, 2), jax.random.fold_in(own_keys[7], 3), 0, NSTRATA - 1).astype(jnp.int32)
    keep = draw_keep(jax.random.fold_in(jax.random.fold_in(splits[11], part), 71), part)
    shard_example_count = draw_shard_example_count(jax.random.fold_in(jax.random.fold_in(splits[11], part), 71), part)
    stratum_owner_table = draw_stratum_owner_table(jax.random.fold_in(splits[11], 71), part)
    return dict(hidden=hidden, cotangent=cotangent, adapter_down_weight=adapter_down_weight, adapter_up_weight=adapter_up_weight, width_projection_factor=width_projection_factor, rank_projection_factor=rank_projection_factor, targets=targets, strata=strata, keep=keep, shard_example_count=shard_example_count, stratum_owner_table=stratum_owner_table)


def per_example(values):
    return values.astype(jnp.float32).reshape(EXAMPLES, SEQ, values.shape[1])

def reference(hidden, cotangent, adapter_down_weight, adapter_up_weight, width_projection_factor, rank_projection_factor, targets, strata, keep, shard_example_count, stratum_owner_table):
    shards = EXAMPLES // EX_DEV
    position = jnp.arange(EXAMPLES, dtype=jnp.int32)
    home_shard = position // EX_DEV
    local_pos = position % EX_DEV
    usable = local_pos < shard_example_count[home_shard]
    is_live = jnp.logical_and(keep == 1, usable)
    counts = jnp.zeros((NSTRATA,), jnp.float32).at[strata].add(is_live.astype(jnp.float32))
    down_activation = jnp.dot(hidden, adapter_down_weight, preferred_element_type=jnp.float32).astype(jnp.bfloat16)
    up_backward_product = jnp.dot(cotangent, adapter_up_weight.T, preferred_element_type=jnp.float32).astype(jnp.bfloat16)
    wide_hidden = jnp.dot(hidden, width_projection_factor, preferred_element_type=jnp.float32).astype(jnp.bfloat16)
    wide_back = jnp.dot(cotangent, width_projection_factor, preferred_element_type=jnp.float32).astype(jnp.bfloat16)
    rank_down = jnp.dot(down_activation, rank_projection_factor, preferred_element_type=jnp.float32).astype(jnp.bfloat16)
    rank_up = jnp.dot(up_backward_product, rank_projection_factor, preferred_element_type=jnp.float32).astype(jnp.bfloat16)
    up_grad = jnp.einsum('esr,esd->erd', per_example(rank_down), per_example(wide_back), precision=lax.Precision.HIGHEST)
    down_grad = jnp.einsum('esd,esr->edr', per_example(wide_hidden), per_example(rank_up), precision=lax.Precision.HIGHEST)
    features = jnp.concatenate([up_grad.reshape(EXAMPLES, KR * KD), down_grad.reshape(EXAMPLES, KD * KR)], axis=1).astype(jnp.bfloat16)
    owner_of = stratum_owner_table[strata]
    owner_blocks = owner_of.reshape(shards, EX_DEV)
    live_blocks = is_live.reshape(shards, EX_DEV)
    ordinal = jnp.arange(EX_DEV, dtype=jnp.int32)
    earlier = ordinal[None, :, None] > ordinal[None, None, :]
    same_owner = owner_blocks[:, :, None] == owner_blocks[:, None, :]
    ahead = jnp.logical_and(jnp.logical_and(earlier, same_owner), live_blocks[:, None, :])
    slot_rank = lax.optimization_barrier(jnp.sum(ahead.astype(jnp.int32), axis=2)).reshape(EXAMPLES)
    is_sent = jnp.logical_and(is_live, slot_rank < CAP)
    bounded_rank = jnp.minimum(slot_rank, CAP - 1)
    slot_owner = jnp.where(is_sent, owner_of, OWNERS)
    slot_table = jnp.zeros((OWNERS, shards, CAP), jnp.int32).at[slot_owner, home_shard, bounded_rank].set(position, mode='drop')
    per_task = TGT // TASKS
    task_mask = ((jnp.arange(TGT, dtype=jnp.int32) // per_task)[:, None] == jnp.arange(TASKS, dtype=jnp.int32)[None, :]).astype(jnp.float32)

    def score_owner(owner_args):
        rows_index, owner_targets = owner_args
        chosen_rows = features[rows_index.reshape(-1)].astype(jnp.float32)
        target_values = owner_targets.astype(jnp.float32)
        row_inv = lax.rsqrt(lax.optimization_barrier(jnp.sum(chosen_rows * chosen_rows, axis=1)) + 1e-06)
        target_inv = lax.rsqrt(lax.optimization_barrier(jnp.sum(target_values * target_values, axis=1)) + 1e-06)
        products = lax.dot_general(chosen_rows, target_values, (((1,), (1,)), ((), ())), precision=lax.Precision.HIGHEST)
        aligned = math.sqrt(FEAT) * products * row_inv[:, None] * target_inv[None, :]
        task_sums = jnp.dot(jnp.maximum(aligned, 0.0), task_mask, precision=lax.Precision.HIGHEST)
        return lax.optimization_barrier(jnp.max(task_sums / per_task, axis=1))
    raw_table = lax.map(score_owner, (slot_table, targets))
    raw_score = raw_table.reshape(OWNERS, shards, CAP)[owner_of, home_shard, bounded_rank]
    stratum_count = counts[strata]
    weight = jnp.sqrt(jnp.sum(counts) / (NSTRATA * jnp.maximum(stratum_count, 1.0)))
    return jnp.where(is_sent, raw_score * weight, 0.0)
```

```python
import functools
import math

import jax
import jax.numpy as jnp
from jax import lax
from jax.experimental import pallas as pl
from jax.experimental.pallas import tpu as pltpu
from jax.sharding import PartitionSpec as P

FEAT = 8192
CAP = 2
TGT = 768
TASKS = 16
SEQ = 8
CORES = 2
LANES = 128
ROW = 1024
PIECES = FEAT // ROW
GROUP = 8
epsilon = 1e-06
bf16, f32, i32 = jnp.bfloat16, jnp.float32, jnp.int32

ANY = pl.BlockSpec(memory_space=pl.ANY)
VMEM = pl.BlockSpec(memory_space=pltpu.VMEM)


def nn(a, b):
    return jnp.dot(a, b, preferred_element_type=f32)


def nt(a, b):
    return lax.dot_general(a, b, (((1,), (1,)), ((), ())), preferred_element_type=f32)


def iota(shape, dim):
    return lax.broadcasted_iota(i32, shape, dim)


def project_kernel(
    strata, keep, present, table, hidden, cotangent, down_t, up, width, rank_t,
    payload, dispatch, member, notes,
    strata_s, keep_s, present_s, table_s, taken, chosen, x, adapters, width_v, rank_v, spread,
    small_sem, row_sem, weight_sem,
):
    examples, strata_total = strata_s.shape[0], table_s.shape[0]
    slots = x.shape[0] // 2
    owners = slots // CAP
    copies = payload.shape[0] // owners
    rank = down_t.shape[0]
    wide = width.shape[1]
    parts = 4
    depth = width.shape[0] // parts

    smalls = [
        pltpu.make_async_copy(a, b, small_sem.at[n])
        for n, (a, b) in enumerate(
            [(strata, strata_s), (keep, keep_s), (present, present_s), (table, table_s)]
        )
    ]
    weights = [
        pltpu.make_async_copy(rank_t, rank_v, weight_sem.at[0]),
        pltpu.make_async_copy(down_t, adapters.at[pl.ds(0, rank)], weight_sem.at[1]),
        pltpu.make_async_copy(up, adapters.at[pl.ds(rank, rank)], weight_sem.at[2]),
    ] + [
        pltpu.make_async_copy(
            width.at[pl.ds(n * depth, depth)], width_v.at[pl.ds(n * depth, depth)], weight_sem.at[3 + n]
        )
        for n in range(parts)
    ]
    for copy in smalls + weights:
        copy.start()

    for n in range(owners):
        taken[n] = 0
    for n in range(slots + 1):
        chosen[n] = 0
    lane = iota((1, LANES), 1)
    for copy in smalls:
        copy.wait()
    counts = jnp.zeros((1, LANES), f32)
    for e in range(examples):
        stratum = strata_s[e]
        live = jnp.where(jnp.logical_and(keep_s[e] == 1, e < present_s[0]), 1, 0)
        owner = table_s[stratum]
        place = taken[owner]
        taken[owner] = place + live
        slot = jnp.where(jnp.logical_and(live == 1, place < CAP), owner * CAP + place, slots)
        chosen[slot] = e
        counts += jnp.where(lane == stratum, live.astype(f32), 0.0)
        member[e : e + 1, :] = (lane == stratum).astype(f32)
        dispatch[e : e + 1, :] = jnp.where(jnp.logical_and(lane == slot, lane < slots), 1.0, 0.0)
    rows = []
    for n in range(slots):
        rows.append(pltpu.make_async_copy(hidden.at[chosen[n]], x.at[n], row_sem.at[n]))
        rows.append(
            pltpu.make_async_copy(cotangent.at[chosen[n]], x.at[slots + n], row_sem.at[slots + n])
        )
    for copy in rows:
        copy.start()

    half = PIECES // 2
    kr = rank_v.shape[0]
    per_row = ROW // wide
    tokens = GROUP * SEQ
    lines = GROUP * half
    spread[...] = (iota((LANES, ROW), 1) // kr == iota((LANES, ROW), 0)).astype(f32).astype(bf16)
    weights[0].wait()
    up_line = iota((per_row * lines, kr), 0)
    pick_up = (per_row * (up_line % half) + up_line // lines == iota((per_row * lines, kr), 1))
    rank_up_rows = nn(pick_up.astype(f32).astype(bf16), rank_v[...]).astype(bf16)
    pick_down = iota((kr * lines, kr), 0) // lines == iota((kr * lines, kr), 1)
    rank_down_rows = nn(pick_down.astype(f32).astype(bf16), rank_v[...]).astype(bf16)
    up_at, up_token = iota((per_row * lines, tokens), 0), iota((per_row * lines, tokens), 1)
    up_mask = (up_at % lines) // half == up_token // SEQ
    down_at, down_token = iota((kr * lines, half * tokens), 0), iota((kr * lines, half * tokens), 1)
    down_mask = jnp.logical_and(
        (down_at % lines) // half == (down_token % tokens) // SEQ, down_at % half == down_token // tokens
    )
    rank_at = iota((lines, ROW), 1) % kr
    for copy in rows + weights[1:3]:
        copy.wait()

    norms = jnp.zeros((1, LANES), f32)
    for g in range(slots // GROUP):
        projected = jnp.zeros((2 * tokens, wide), f32)
        adapted = jnp.zeros((2 * tokens, 2 * rank), f32)
        for n in range(parts):
            span = pl.ds(n * depth, depth)
            both = jnp.concatenate(
                [
                    x[g * GROUP : (g + 1) * GROUP, :, span].reshape(tokens, depth),
                    x[slots + g * GROUP : slots + (g + 1) * GROUP, :, span].reshape(tokens, depth),
                ],
                axis=0,
            )
            adapted += nt(both, adapters[:, span])
            if g == 0:
                weights[3 + n].wait()
            projected += nn(both, width_v[span, :])
        down_act = adapted[:tokens, :rank].astype(bf16)
        up_back = adapted[tokens:, rank:].astype(bf16)
        wide_hidden = projected[:tokens].astype(bf16)
        wide_back = projected[tokens:].astype(bf16)

        left = jnp.where(up_mask, nt(rank_up_rows, down_act), 0.0).astype(bf16)
        up_grad = nn(left, wide_back)
        up_rows = jnp.concatenate(
            [up_grad[n * lines : (n + 1) * lines] for n in range(per_row)], axis=1
        ).astype(bf16)

        left = nt(rank_down_rows, jnp.concatenate([up_back] * half, axis=0))
        left = jnp.where(down_mask, left, 0.0).astype(bf16)
        stacked = jnp.concatenate(
            [wide_hidden[:, n * LANES : (n + 1) * LANES] for n in range(half)], axis=0
        )
        down_grad = nn(left, stacked).astype(bf16)
        repeated = nn(down_grad, spread[...])
        down_rows = repeated[:lines]
        for n in range(1, kr):
            down_rows = jnp.where(rank_at == n, repeated[n * lines : (n + 1) * lines], down_rows)

        up_rows = up_rows.astype(f32)
        squares = jnp.sum(up_rows * up_rows + down_rows * down_rows, axis=1, keepdims=True)
        slot_of = g * GROUP + iota((lines, LANES), 0) // half
        norms += jnp.sum(
            jnp.where(slot_of == iota((lines, LANES), 1), squares, 0.0), axis=0, keepdims=True
        )
        per_owner = CAP * half
        for n in range(GROUP // CAP):
            owner = g * (GROUP // CAP) + n
            piece = jnp.concatenate(
                [
                    up_rows[n * per_owner : (n + 1) * per_owner],
                    down_rows[n * per_owner : (n + 1) * per_owner],
                ],
                axis=0,
            ).astype(bf16)
            for c in range(copies):
                payload[owner * copies + c] = piece
    notes[...] = jnp.concatenate(
        [lax.rsqrt(norms + epsilon), counts, jnp.zeros((6, LANES), f32)], axis=0
    )


def target_kernel(targets, stacked, inverse, sem):
    copies = [
        pltpu.make_async_copy(
            targets.at[0, :, pl.ds(n * ROW, ROW)], stacked.at[n], sem.at[n]
        )
        for n in range(PIECES)
    ]
    for copy in copies:
        copy.start()
    total = jnp.zeros((targets.shape[1], LANES), f32)
    for n in range(PIECES):
        copies[n].wait()
        for m in range(ROW // LANES):
            part = stacked[n, :, m * LANES : (m + 1) * LANES].astype(f32)
            total += part * part
    scale = math.sqrt(FEAT) / (TGT // TASKS)
    inverse[...] = jnp.broadcast_to(
        scale * lax.rsqrt(jnp.sum(total, axis=1, keepdims=True) + epsilon), inverse.shape
    )


def score_kernel(stacked, inverse, mine, other, notes, back):
    per_task = TGT // TASKS
    half = PIECES // 2
    sources = LANES // (CAP * PIECES)
    own_core = lax.axis_index("core")
    first = lax.axis_index("dp") * CAP
    share = stacked.shape[1]
    line = iota((1, CORES * LANES), 1)
    piece_of = (line // (CAP * half)) % 2 * half + line % half
    inv = inverse[...]
    dst = iota((CORES * sources, LANES), 0)
    lane = iota((CORES * sources, LANES), 1)
    for b in range(mine.shape[0] // sources):
        block = jnp.concatenate(
            [
                mine[b * sources : (b + 1) * sources].reshape(LANES, ROW),
                other[b * sources : (b + 1) * sources].reshape(LANES, ROW),
            ],
            axis=0,
        )
        products = nt(stacked[0], block)
        for n in range(1, PIECES):
            products = jnp.where(piece_of == n, nt(stacked[n], block), products)
        best = []
        for c in range(CORES):
            total = products[:, c * LANES : (c + 1) * LANES]
            for shift in (1, 2, CAP * half):
                total = total + pltpu.roll(total, LANES - shift, 1)
            total = jnp.maximum(total, 0.0) * inv
            top = jnp.sum(total[:per_task], axis=0, keepdims=True)
            for n in range(1, share // per_task):
                top = jnp.maximum(
                    top, jnp.sum(total[n * per_task : (n + 1) * per_task], axis=0, keepdims=True)
                )
            best.append(top)
        table = jnp.where(dst % CORES == own_core, best[0], best[1])
        scores = jnp.zeros((CORES * sources, LANES), f32)
        for n in range(CAP):
            at = lane == dst // CORES * (CAP * PIECES) + n * half
            column = jnp.sum(jnp.where(at, table, 0.0), axis=1, keepdims=True)
            scores = jnp.where(lane == first + n, column, scores)
        for n in range(CORES * sources):
            back[b * CORES * sources + n] = jnp.concatenate(
                [scores[n : n + 1], notes[1:2, :]], axis=1
            )


def finish_kernel(strata_total, returned, dispatch, member, notes, out):
    values = returned[:, 0, :]
    raw = jnp.max(values[:, :LANES], axis=0, keepdims=True) * notes[0:1, :]
    counts = jnp.sum(values[:, LANES:], axis=0, keepdims=True)
    live = jnp.sum(counts, axis=1, keepdims=True)
    weight = jnp.sqrt(live / (strata_total * jnp.maximum(counts, 1.0)))
    picked = jnp.sum(dispatch[...] * raw, axis=1, keepdims=True)
    picked = picked * jnp.sum(member[...] * weight, axis=1, keepdims=True)
    examples = dispatch.shape[0]
    square = iota((examples, LANES), 0) == iota((examples, LANES), 1)
    out[...] = jnp.sum(jnp.where(square, picked, 0.0), axis=0)[:examples]


def shards(
    hidden,
    cotangent,
    adapter_down_weight,
    adapter_up_weight,
    width_projection_factor,
    rank_projection_factor,
    targets,
    strata,
    keep,
    shard_example_count,
    stratum_owner_table,
):
    examples = strata.shape[0]
    strata_total = stratum_owner_table.shape[0]
    owners, columns = lax.axis_size("dp"), lax.axis_size("x")
    slots = owners * CAP
    model, wide = width_projection_factor.shape
    rank, kr = rank_projection_factor.shape
    share = targets.shape[1]
    chips = owners * columns

    payload, dispatch, member, notes = pl.pallas_call(
        project_kernel,
        out_shape=(
            jax.ShapeDtypeStruct((chips, CAP * PIECES, ROW), bf16),
            jax.ShapeDtypeStruct((examples, LANES), f32),
            jax.ShapeDtypeStruct((examples, LANES), f32),
            jax.ShapeDtypeStruct((8, LANES), f32),
        ),
        in_specs=[ANY] * 10,
        out_specs=(VMEM,) * 4,
        scratch_shapes=[
            pltpu.SMEM((examples,), i32),
            pltpu.SMEM((examples,), i32),
            pltpu.SMEM((1,), i32),
            pltpu.SMEM((strata_total,), i32),
            pltpu.SMEM((owners,), i32),
            pltpu.SMEM((slots + 1,), i32),
            pltpu.VMEM((2 * slots, SEQ, model), bf16),
            pltpu.VMEM((2 * rank, model), bf16),
            pltpu.VMEM((model, wide), bf16),
            pltpu.VMEM((kr, rank), bf16),
            pltpu.VMEM((LANES, ROW), bf16),
            pltpu.SemaphoreType.DMA((4,)),
            pltpu.SemaphoreType.DMA((2 * slots,)),
            pltpu.SemaphoreType.DMA((7,)),
        ],
        compiler_params=pltpu.CompilerParams(vmem_limit_bytes=40 * 2**20),
        name="project",
    )(
        strata,
        keep,
        shard_example_count,
        stratum_owner_table,
        hidden.reshape(examples, SEQ, model),
        cotangent.reshape(examples, SEQ, model),
        adapter_down_weight.T,
        adapter_up_weight,
        width_projection_factor,
        rank_projection_factor.T,
    )
    stacked, inverse = pl.pallas_call(
        target_kernel,
        out_shape=(
            jax.ShapeDtypeStruct((PIECES, share, ROW), bf16),
            jax.ShapeDtypeStruct((share, LANES), f32),
        ),
        in_specs=[ANY],
        out_specs=(VMEM, VMEM),
        scratch_shapes=[pltpu.SemaphoreType.DMA((PIECES,))],
        compiler_params=pltpu.CompilerParams(vmem_limit_bytes=20 * 2**20),
        cost_estimate=pl.CostEstimate(flops=4 * share * FEAT, bytes_accessed=4 * share * FEAT, transcendentals=0),
        name="target_norms",
    )(targets)
    mine = lax.all_to_all(payload, ("dp", "x"), split_axis=0, concat_axis=0, tiled=True)
    other = lax.ppermute(mine, "core", [(n, (n + 1) % CORES) for n in range(CORES)])
    back = pl.pallas_call(
        score_kernel,
        out_shape=jax.ShapeDtypeStruct((chips * CORES, 1, 2 * LANES), f32),
        in_specs=[VMEM] * 5,
        out_specs=VMEM,
        compiler_params=pltpu.CompilerParams(vmem_limit_bytes=40 * 2**20),
        name="score",
    )(stacked, inverse, mine, other, notes)
    returned = lax.all_to_all(back, ("dp", "x", "core"), split_axis=0, concat_axis=0, tiled=True)
    return pl.pallas_call(
        functools.partial(finish_kernel, strata_total),
        out_shape=jax.ShapeDtypeStruct((examples,), f32),
        in_specs=[VMEM] * 4,
        out_specs=VMEM,
        name="finish",
    )(returned, dispatch, member, notes)


def solution(mesh):
    sizes = [mesh.shape[name] for name in ("groups", "dp", "tgt")]
    fine = jax.sharding.Mesh(
        mesh.devices.reshape(sizes[0], sizes[1], sizes[2] // CORES, CORES),
        ("groups", "dp", "x", "core"),
    )
    every = P(("groups", "dp", "x", "core"))
    whole = P()
    return jax.shard_map(
        shards,
        mesh=fine,
        in_specs=(
            every, every, whole, whole, whole, whole,
            P(("groups", "dp"), ("x", "core"), None),
            every, every, every, whole,
        ),
        out_specs=every,
        check_vma=False,
    )
```

```python
import functools
import math

import jax
import jax.numpy as jnp
from jax import lax
from jax.experimental import pallas as pl
from jax.experimental.pallas import tpu as pltpu
from jax.sharding import PartitionSpec as P

FEAT = 8192
CAP = 2
TGT = 768
TASKS = 16
SEQ = 8
CORES = 2
LANES = 128
ROW = 1024
PIECES = FEAT // ROW
GROUP = 8
epsilon = 1e-06
bf16, f32, i32 = jnp.bfloat16, jnp.float32, jnp.int32

HBM = pl.BlockSpec(memory_space=pltpu.HBM)
VMEM = pl.BlockSpec(memory_space=pltpu.VMEM)


def nn(a, b):
    return jnp.dot(a, b, preferred_element_type=f32)


def nt(a, b):
    return lax.dot_general(a, b, (((1,), (1,)), ((), ())), preferred_element_type=f32)


def in_hbm(*arrays):
    return [pltpu.with_memory_space_constraint(a, pltpu.HBM) for a in arrays]


def iota(shape, dim):
    return lax.broadcasted_iota(i32, shape, dim)


def project_kernel(
    present, strata, keep, table, hidden, cotangent, down_t, up, width, rank_t,
    payload, dispatch, member, notes,
    strata_s, keep_s, table_s, taken, chosen, x, adapters, width_v, rank_v, spread,
    small_sem, row_sem, weight_sem,
):
    examples, strata_total = strata_s.shape[0], table_s.shape[0]
    slots = x.shape[0] // 2
    owners = slots // CAP
    copies = payload.shape[0] // owners
    rank = down_t.shape[0]
    wide = width.shape[1]
    parts = 4
    depth = width.shape[0] // parts

    smalls = [
        pltpu.make_async_copy(a, b, small_sem.at[n])
        for n, (a, b) in enumerate(
            [(strata, strata_s), (keep, keep_s), (table, table_s)]
        )
    ]
    weights = [
        pltpu.make_async_copy(rank_t, rank_v, weight_sem.at[0]),
        pltpu.make_async_copy(down_t, adapters.at[pl.ds(0, rank)], weight_sem.at[1]),
        pltpu.make_async_copy(up, adapters.at[pl.ds(rank, rank)], weight_sem.at[2]),
    ] + [
        pltpu.make_async_copy(
            width.at[pl.ds(n * depth, depth)], width_v.at[pl.ds(n * depth, depth)], weight_sem.at[3 + n]
        )
        for n in range(parts)
    ]
    for copy in smalls + weights:
        copy.start()

    for n in range(owners):
        taken[n] = 0
    for n in range(slots + 1):
        chosen[n] = 0
    lane = iota((1, LANES), 1)
    for copy in smalls:
        copy.wait()
    counts = jnp.zeros((1, LANES), f32)
    for e in range(examples):
        stratum = strata_s[e]
        live = jnp.where(jnp.logical_and(keep_s[e] == 1, e < present[0]), 1, 0)
        owner = table_s[stratum]
        place = taken[owner]
        taken[owner] = place + live
        slot = jnp.where(jnp.logical_and(live == 1, place < CAP), owner * CAP + place, slots)
        chosen[slot] = e
        counts += jnp.where(lane == stratum, live.astype(f32), 0.0)
        member[e : e + 1, :] = (lane == stratum).astype(f32)
        dispatch[e : e + 1, :] = jnp.where(jnp.logical_and(lane == slot, lane < slots), 1.0, 0.0)
    rows = []
    for n in range(slots):
        rows.append(pltpu.make_async_copy(hidden.at[chosen[n]], x.at[n], row_sem.at[n]))
        rows.append(
            pltpu.make_async_copy(cotangent.at[chosen[n]], x.at[slots + n], row_sem.at[slots + n])
        )
    for copy in rows:
        copy.start()

    half = PIECES // 2
    kr = rank_v.shape[0]
    per_row = ROW // wide
    tokens = GROUP * SEQ
    lines = GROUP * half
    spread[...] = (iota((LANES, ROW), 1) // kr == iota((LANES, ROW), 0)).astype(f32).astype(bf16)
    weights[0].wait()
    up_line = iota((per_row * lines, kr), 0)
    pick_up = (per_row * (up_line % half) + up_line // lines == iota((per_row * lines, kr), 1))
    rank_up_rows = nn(pick_up.astype(f32).astype(bf16), rank_v[...]).astype(bf16)
    pick_down = iota((kr * lines, kr), 0) // lines == iota((kr * lines, kr), 1)
    rank_down_rows = nn(pick_down.astype(f32).astype(bf16), rank_v[...]).astype(bf16)
    up_at, up_token = iota((per_row * lines, tokens), 0), iota((per_row * lines, tokens), 1)
    up_mask = (up_at % lines) // half == up_token // SEQ
    down_at, down_token = iota((kr * lines, half * tokens), 0), iota((kr * lines, half * tokens), 1)
    down_mask = jnp.logical_and(
        (down_at % lines) // half == (down_token % tokens) // SEQ, down_at % half == down_token // tokens
    )
    rank_at = iota((lines, ROW), 1) % kr
    for copy in rows + weights[1:3]:
        copy.wait()

    norms = jnp.zeros((1, LANES), f32)
    for g in range(slots // GROUP):
        projected = jnp.zeros((2 * tokens, wide), f32)
        adapted = jnp.zeros((2 * tokens, 2 * rank), f32)
        for n in range(parts):
            span = pl.ds(n * depth, depth)
            both = jnp.concatenate(
                [
                    x[g * GROUP : (g + 1) * GROUP, :, span].reshape(tokens, depth),
                    x[slots + g * GROUP : slots + (g + 1) * GROUP, :, span].reshape(tokens, depth),
                ],
                axis=0,
            )
            adapted += nt(both, adapters[:, span])
            if g == 0:
                weights[3 + n].wait()
            projected += nn(both, width_v[span, :])
        down_act = adapted[:tokens, :rank].astype(bf16)
        up_back = adapted[tokens:, rank:].astype(bf16)
        wide_hidden = projected[:tokens].astype(bf16)
        wide_back = projected[tokens:].astype(bf16)

        left = jnp.where(up_mask, nt(rank_up_rows, down_act), 0.0).astype(bf16)
        up_grad = nn(left, wide_back)
        up_rows = jnp.concatenate(
            [up_grad[n * lines : (n + 1) * lines] for n in range(per_row)], axis=1
        ).astype(bf16)

        left = nt(rank_down_rows, jnp.concatenate([up_back] * half, axis=0))
        left = jnp.where(down_mask, left, 0.0).astype(bf16)
        stacked = jnp.concatenate(
            [wide_hidden[:, n * LANES : (n + 1) * LANES] for n in range(half)], axis=0
        )
        down_grad = nn(left, stacked).astype(bf16)
        repeated = nn(down_grad, spread[...])
        down_rows = repeated[:lines]
        for n in range(1, kr):
            down_rows = jnp.where(rank_at == n, repeated[n * lines : (n + 1) * lines], down_rows)

        up_rows = up_rows.astype(f32)
        squares = jnp.sum(up_rows * up_rows + down_rows * down_rows, axis=1, keepdims=True)
        slot_of = g * GROUP + iota((lines, LANES), 0) // half
        norms += jnp.sum(
            jnp.where(slot_of == iota((lines, LANES), 1), squares, 0.0), axis=0, keepdims=True
        )
        per_owner = CAP * half
        for n in range(GROUP // CAP):
            owner = g * (GROUP // CAP) + n
            piece = jnp.concatenate(
                [
                    up_rows[n * per_owner : (n + 1) * per_owner],
                    down_rows[n * per_owner : (n + 1) * per_owner],
                ],
                axis=0,
            ).astype(bf16)
            for c in range(copies):
                payload[owner * copies + c] = piece
    notes[...] = jnp.concatenate(
        [lax.rsqrt(norms + epsilon), counts, jnp.zeros((6, LANES), f32)], axis=0
    )


def target_kernel(targets, stacked, inverse, sem):
    copies = [
        pltpu.make_async_copy(
            targets.at[0, :, pl.ds(n * ROW, ROW)], stacked.at[n], sem.at[n]
        )
        for n in range(PIECES)
    ]
    for copy in copies:
        copy.start()
    total = jnp.zeros((targets.shape[1], LANES), f32)
    for n in range(PIECES):
        copies[n].wait()
        for m in range(ROW // LANES):
            part = stacked[n, :, m * LANES : (m + 1) * LANES].astype(f32)
            total += part * part
    scale = math.sqrt(FEAT) / (TGT // TASKS)
    inverse[...] = jnp.broadcast_to(
        scale * lax.rsqrt(jnp.sum(total, axis=1, keepdims=True) + epsilon), inverse.shape
    )


def score_kernel(stacked, inverse, mine, other, notes, back):
    per_task = TGT // TASKS
    half = PIECES // 2
    sources = LANES // (CAP * PIECES)
    own_core = lax.axis_index("core")
    first = lax.axis_index("dp") * CAP
    share = stacked.shape[1]
    line = iota((1, CORES * LANES), 1)
    piece_of = (line // (CAP * half)) % 2 * half + line % half
    inv = inverse[...]
    dst = iota((CORES * sources, LANES), 0)
    lane = iota((CORES * sources, LANES), 1)
    for b in range(mine.shape[0] // sources):
        block = jnp.concatenate(
            [
                mine[b * sources : (b + 1) * sources].reshape(LANES, ROW),
                other[b * sources : (b + 1) * sources].reshape(LANES, ROW),
            ],
            axis=0,
        )
        products = nt(stacked[0], block)
        for n in range(1, PIECES):
            products = jnp.where(piece_of == n, nt(stacked[n], block), products)
        best = []
        for c in range(CORES):
            total = products[:, c * LANES : (c + 1) * LANES]
            for shift in (1, 2, CAP * half):
                total = total + pltpu.roll(total, LANES - shift, 1)
            total = jnp.maximum(total, 0.0) * inv
            top = jnp.sum(total[:per_task], axis=0, keepdims=True)
            for n in range(1, share // per_task):
                top = jnp.maximum(
                    top, jnp.sum(total[n * per_task : (n + 1) * per_task], axis=0, keepdims=True)
                )
            best.append(top)
        table = jnp.where(dst % CORES == own_core, best[0], best[1])
        scores = jnp.zeros((CORES * sources, LANES), f32)
        for n in range(CAP):
            at = lane == dst // CORES * (CAP * PIECES) + n * half
            column = jnp.sum(jnp.where(at, table, 0.0), axis=1, keepdims=True)
            scores = jnp.where(lane == first + n, column, scores)
        for n in range(CORES * sources):
            back[b * CORES * sources + n] = jnp.concatenate(
                [scores[n : n + 1], notes[1:2, :]], axis=1
            )


def finish_kernel(strata_total, returned, dispatch, member, notes, out):
    values = returned[:, 0, :]
    raw = jnp.max(values[:, :LANES], axis=0, keepdims=True) * notes[0:1, :]
    counts = jnp.sum(values[:, LANES:], axis=0, keepdims=True)
    live = jnp.sum(counts, axis=1, keepdims=True)
    weight = jnp.sqrt(live / (strata_total * jnp.maximum(counts, 1.0)))
    picked = jnp.sum(dispatch[...] * raw, axis=1, keepdims=True)
    picked = picked * jnp.sum(member[...] * weight, axis=1, keepdims=True)
    examples = dispatch.shape[0]
    square = iota((examples, LANES), 0) == iota((examples, LANES), 1)
    out[...] = jnp.sum(jnp.where(square, picked, 0.0), axis=0)[:examples]


def shards(
    hidden,
    cotangent,
    adapter_down_weight,
    adapter_up_weight,
    width_projection_factor,
    rank_projection_factor,
    targets,
    strata,
    keep,
    shard_example_count,
    stratum_owner_table,
):
    examples = strata.shape[0]
    strata_total = stratum_owner_table.shape[0]
    owners, columns = lax.axis_size("dp"), lax.axis_size("x")
    slots = owners * CAP
    model, wide = width_projection_factor.shape
    rank, kr = rank_projection_factor.shape
    share = targets.shape[1]
    chips = owners * columns

    payload, dispatch, member, notes = pl.pallas_call(
        project_kernel,
        out_shape=(
            jax.ShapeDtypeStruct((chips, CAP * PIECES, ROW), bf16),
            jax.ShapeDtypeStruct((examples, LANES), f32),
            jax.ShapeDtypeStruct((examples, LANES), f32),
            jax.ShapeDtypeStruct((8, LANES), f32),
        ),
        in_specs=[pl.BlockSpec(memory_space=pltpu.SMEM)] + [HBM] * 9,
        out_specs=(VMEM,) * 4,
        scratch_shapes=[
            pltpu.SMEM((examples,), i32),
            pltpu.SMEM((examples,), i32),
            pltpu.SMEM((strata_total,), i32),
            pltpu.SMEM((owners,), i32),
            pltpu.SMEM((slots + 1,), i32),
            pltpu.VMEM((2 * slots, SEQ, model), bf16),
            pltpu.VMEM((2 * rank, model), bf16),
            pltpu.VMEM((model, wide), bf16),
            pltpu.VMEM((kr, rank), bf16),
            pltpu.VMEM((LANES, ROW), bf16),
            pltpu.SemaphoreType.DMA((3,)),
            pltpu.SemaphoreType.DMA((2 * slots,)),
            pltpu.SemaphoreType.DMA((7,)),
        ],
        compiler_params=pltpu.CompilerParams(vmem_limit_bytes=40 * 2**20),
        name="project",
    )(
        shard_example_count,
        *in_hbm(
            strata,
            keep,
            stratum_owner_table,
            hidden.reshape(examples, SEQ, model),
            cotangent.reshape(examples, SEQ, model),
            adapter_down_weight.T,
            adapter_up_weight,
            width_projection_factor,
            rank_projection_factor.T,
        )
    )
    stacked, inverse = pl.pallas_call(
        target_kernel,
        out_shape=(
            jax.ShapeDtypeStruct((PIECES, share, ROW), bf16),
            jax.ShapeDtypeStruct((share, LANES), f32),
        ),
        in_specs=[HBM],
        out_specs=(VMEM, VMEM),
        scratch_shapes=[pltpu.SemaphoreType.DMA((PIECES,))],
        compiler_params=pltpu.CompilerParams(vmem_limit_bytes=20 * 2**20),
        cost_estimate=pl.CostEstimate(flops=4 * share * FEAT, bytes_accessed=4 * share * FEAT, transcendentals=0),
        name="target_norms",
    )(*in_hbm(targets))
    mine = lax.all_to_all(payload, ("dp", "x"), split_axis=0, concat_axis=0, tiled=True)
    other = lax.ppermute(mine, "core", [(n, (n + 1) % CORES) for n in range(CORES)])
    back = pl.pallas_call(
        score_kernel,
        out_shape=jax.ShapeDtypeStruct((chips * CORES, 1, 2 * LANES), f32),
        in_specs=[VMEM] * 5,
        out_specs=VMEM,
        compiler_params=pltpu.CompilerParams(vmem_limit_bytes=40 * 2**20),
        name="score",
    )(stacked, inverse, mine, other, notes)
    returned = lax.all_to_all(back, ("dp", "x", "core"), split_axis=0, concat_axis=0, tiled=True)
    return pl.pallas_call(
        functools.partial(finish_kernel, strata_total),
        out_shape=jax.ShapeDtypeStruct((examples,), f32),
        in_specs=[VMEM] * 4,
        out_specs=VMEM,
        name="finish",
    )(returned, dispatch, member, notes)


def solution(mesh):
    sizes = [mesh.shape[name] for name in ("groups", "dp", "tgt")]
    fine = jax.sharding.Mesh(
        mesh.devices.reshape(sizes[0], sizes[1], sizes[2] // CORES, CORES),
        ("groups", "dp", "x", "core"),
    )
    every = P(("groups", "dp", "x", "core"))
    whole = P()
    return jax.shard_map(
        shards,
        mesh=fine,
        in_specs=(
            every, every, whole, whole, whole, whole,
            P(("groups", "dp"), ("x", "core"), None),
            every, every, every, whole,
        ),
        out_specs=every,
        check_vma=False,
    )
```

```python
import functools
import math

import jax
import jax.numpy as jnp
from jax import lax
from jax.experimental import pallas as pl
from jax.experimental.pallas import tpu as pltpu
from jax.sharding import PartitionSpec as P

FEAT = 8192
CAP = 2
TGT = 768
TASKS = 16
SEQ = 8
CORES = 2
LANES = 128
ROW = 1024
PIECES = FEAT // ROW
GROUP = 8
epsilon = 1e-06
bf16, f32, i32 = jnp.bfloat16, jnp.float32, jnp.int32

HBM = pl.BlockSpec(memory_space=pltpu.HBM)
VMEM = pl.BlockSpec(memory_space=pltpu.VMEM)


def nn(a, b):
    return jnp.dot(a, b, preferred_element_type=f32)


def nt(a, b):
    return lax.dot_general(a, b, (((1,), (1,)), ((), ())), preferred_element_type=f32)


def in_hbm(*arrays):
    return [pltpu.with_memory_space_constraint(a, pltpu.HBM) for a in arrays]


def iota(shape, dim):
    return lax.broadcasted_iota(i32, shape, dim)


def project_kernel(
    present, strata, keep, table, hidden, cotangent, down_t, up, width, rank_t,
    payload, dispatch, member, notes,
    strata_s, keep_s, table_s, taken, chosen, x, adapters, adapters_t, width_v, rank_v, spread,
    small_sem, row_sem, weight_sem,
):
    examples, strata_total = strata_s.shape[0], table_s.shape[0]
    slots = x.shape[0] // 2
    owners = slots // CAP
    copies = payload.shape[0] // owners
    rank = down_t.shape[0]
    wide = width.shape[1]
    parts = 2
    early = 1
    depth = width.shape[0] // parts

    smalls = [
        pltpu.make_async_copy(a, b, small_sem.at[n])
        for n, (a, b) in enumerate(
            [(strata, strata_s), (keep, keep_s), (table, table_s)]
        )
    ]
    weights = [
        pltpu.make_async_copy(rank_t, rank_v, weight_sem.at[0]),
        pltpu.make_async_copy(down_t, adapters.at[pl.ds(0, rank)], weight_sem.at[1]),
        pltpu.make_async_copy(up, adapters.at[pl.ds(rank, rank)], weight_sem.at[2]),
    ] + [
        pltpu.make_async_copy(
            width.at[pl.ds(n * depth, depth)], width_v.at[pl.ds(n * depth, depth)], weight_sem.at[3 + n]
        )
        for n in range(parts)
    ]
    for copy in smalls + weights[: 3 + early]:
        copy.start()

    for n in range(owners):
        taken[n] = 0
    for n in range(slots + 1):
        chosen[n] = 0
    lane = iota((1, notes.shape[1]), 1)
    for copy in smalls:
        copy.wait()
    counts = jnp.zeros(lane.shape, f32)
    for e in range(examples):
        stratum = strata_s[e]
        live = jnp.where(jnp.logical_and(keep_s[e] == 1, e < present[0]), 1, 0)
        owner = table_s[stratum]
        place = taken[owner]
        taken[owner] = place + live
        slot = jnp.where(jnp.logical_and(live == 1, place < CAP), owner * CAP + place, slots)
        chosen[slot] = e
        counts += jnp.where(lane == slots + stratum, live.astype(f32), 0.0)
        member[e : e + 1, :] = (lane == slots + stratum).astype(f32)
        dispatch[e : e + 1, :] = jnp.where(jnp.logical_and(lane == slot, lane < slots), 1.0, 0.0)
    rows = []
    for n in range(slots):
        rows.append(pltpu.make_async_copy(hidden.at[chosen[n]], x.at[n], row_sem.at[n]))
        rows.append(
            pltpu.make_async_copy(cotangent.at[chosen[n]], x.at[slots + n], row_sem.at[slots + n])
        )
    for copy in rows + weights[3 + early :]:
        copy.start()

    half = PIECES // 2
    kr = rank_v.shape[0]
    per_row = ROW // wide
    tokens = GROUP * SEQ
    lines = GROUP * half
    spread[...] = (iota((LANES, ROW), 1) // kr == iota((LANES, ROW), 0)).astype(f32).astype(bf16)
    weights[0].wait()
    up_line = iota((per_row * lines, kr), 0)
    pick_up = (per_row * (up_line % half) + up_line // lines == iota((per_row * lines, kr), 1))
    rank_up_rows = nn(pick_up.astype(f32).astype(bf16), rank_v[...]).astype(bf16)
    pick_down = iota((kr * lines, kr), 0) // lines == iota((kr * lines, kr), 1)
    rank_down_rows = nn(pick_down.astype(f32).astype(bf16), rank_v[...]).astype(bf16)
    up_at, up_token = iota((per_row * lines, tokens), 0), iota((per_row * lines, tokens), 1)
    up_mask = (up_at % lines) // half == up_token // SEQ
    down_at, down_token = iota((kr * lines, half * tokens), 0), iota((kr * lines, half * tokens), 1)
    down_mask = jnp.logical_and(
        (down_at % lines) // half == (down_token % tokens) // SEQ, down_at % half == down_token // tokens
    )
    rank_at = iota((lines, ROW), 1) % kr
    for copy in weights[1:3]:
        copy.wait()
    adapters_t[...] = adapters[...].T
    for copy in rows:
        copy.wait()

    norms = jnp.zeros(lane.shape, f32)
    for g in range(slots // GROUP):
        model = x.shape[2]
        def both(lo, size):
            return jnp.concatenate(
                [
                    x[g * GROUP : (g + 1) * GROUP, :, lo : lo + size].reshape(tokens, size),
                    x[slots + g * GROUP : slots + (g + 1) * GROUP, :, lo : lo + size].reshape(tokens, size),
                ],
                axis=0,
            )

        adapted = nn(both(0, model), adapters_t[...])
        for n in range(parts):
            if g == 0:
                weights[3 + n].wait()
            span = pl.ds(n * depth, depth)
            part = nn(both(n * depth, depth), width_v[span, :])
            projected = part if n == 0 else projected + part
        down_act = adapted[:tokens, :rank].astype(bf16)
        up_back = adapted[tokens:, rank:].astype(bf16)
        wide_hidden = projected[:tokens].astype(bf16)
        wide_back = projected[tokens:].astype(bf16)

        left = jnp.where(up_mask, nt(rank_up_rows, down_act), 0.0).astype(bf16)
        up_grad = nn(left, wide_back)
        up_rows = jnp.concatenate(
            [up_grad[n * lines : (n + 1) * lines] for n in range(per_row)], axis=1
        ).astype(bf16)

        left = nt(rank_down_rows, jnp.concatenate([up_back] * half, axis=0))
        left = jnp.where(down_mask, left, 0.0).astype(bf16)
        stacked = jnp.concatenate(
            [wide_hidden[:, n * LANES : (n + 1) * LANES] for n in range(half)], axis=0
        )
        down_grad = nn(left, stacked).astype(bf16)
        repeated = nn(down_grad, spread[...])
        down_rows = repeated[:lines]
        for n in range(1, kr):
            down_rows = jnp.where(rank_at == n, repeated[n * lines : (n + 1) * lines], down_rows)

        up_rows = up_rows.astype(f32)
        squares = jnp.sum(up_rows * up_rows + down_rows * down_rows, axis=1, keepdims=True)
        at = (lines, notes.shape[1])
        slot_of = g * GROUP + iota(at, 0) // half
        norms += jnp.sum(jnp.where(slot_of == iota(at, 1), squares, 0.0), axis=0, keepdims=True)
        per_owner = CAP * half
        for n in range(GROUP // CAP):
            owner = g * (GROUP // CAP) + n
            piece = jnp.concatenate(
                [
                    up_rows[n * per_owner : (n + 1) * per_owner],
                    down_rows[n * per_owner : (n + 1) * per_owner],
                ],
                axis=0,
            ).astype(bf16)
            for c in range(copies):
                payload[c * owners + owner] = piece
    notes[...] = jnp.concatenate(
        [lax.rsqrt(norms + epsilon), counts, jnp.zeros((6, notes.shape[1]), f32)], axis=0
    )


def target_kernel(targets, stacked, inverse, sem):
    copies = [
        pltpu.make_async_copy(
            targets.at[0, :, pl.ds(n * ROW, ROW)], stacked.at[n], sem.at[n]
        )
        for n in range(PIECES)
    ]
    for copy in copies:
        copy.start()
    total = jnp.zeros((targets.shape[1], LANES), f32)
    for n in range(PIECES):
        copies[n].wait()
        for m in range(ROW // LANES):
            part = stacked[n, :, m * LANES : (m + 1) * LANES].astype(f32)
            total += part * part
    scale = math.sqrt(FEAT) / (TGT // TASKS)
    inverse[...] = jnp.broadcast_to(
        scale * lax.rsqrt(jnp.sum(total, axis=1, keepdims=True) + epsilon), inverse.shape
    )


def score_kernel(stacked, inverse, mine, other, notes, back):
    per_task = TGT // TASKS
    half = PIECES // 2
    sources = LANES // (CAP * PIECES)
    own_core = lax.axis_index("core")
    first = lax.axis_index("dp") * CAP
    share = stacked.shape[1]
    line = iota((1, CORES * LANES), 1)
    piece_of = (line // (CAP * half)) % 2 * half + line % half
    inv = inverse[...]
    dst = iota((CORES * sources, LANES), 0)
    lane = iota((CORES * sources, LANES), 1)
    for b in range(mine.shape[0] // sources):
        block = jnp.concatenate(
            [
                mine[b * sources : (b + 1) * sources].reshape(LANES, ROW),
                other[b * sources : (b + 1) * sources].reshape(LANES, ROW),
            ],
            axis=0,
        )
        whole = nt(stacked[...].reshape(PIECES * share, ROW), block)
        products = whole[:share]
        for n in range(1, PIECES):
            products = jnp.where(piece_of == n, whole[n * share : (n + 1) * share], products)
        best = []
        for c in range(CORES):
            total = products[:, c * LANES : (c + 1) * LANES]
            for shift in (1, 2, CAP * half):
                total = total + pltpu.roll(total, LANES - shift, 1)
            total = jnp.maximum(total, 0.0) * inv
            top = jnp.sum(total[:per_task], axis=0, keepdims=True)
            for n in range(1, share // per_task):
                top = jnp.maximum(
                    top, jnp.sum(total[n * per_task : (n + 1) * per_task], axis=0, keepdims=True)
                )
            best.append(top)
        table = jnp.where(dst % CORES == own_core, best[0], best[1])
        scores = jnp.broadcast_to(notes[1:2, :], (CORES * sources, notes.shape[1]))
        for n in range(CAP):
            at = lane == dst // CORES * (CAP * PIECES) + n * half
            column = jnp.sum(jnp.where(at, table, 0.0), axis=1, keepdims=True)
            scores = jnp.where(iota(scores.shape, 1) == first + n, column, scores)
        for n in range(CORES * sources):
            back[b * CORES * sources + n] = scores[n : n + 1]


def finish_kernel(slots, strata_total, returned, dispatch, member, notes, out):
    values = returned[:, 0, :]
    raw = jnp.max(values, axis=0, keepdims=True) * notes[0:1, :]
    counts = jnp.sum(values, axis=0, keepdims=True)
    held = iota(counts.shape, 1)
    held = jnp.logical_and(held >= slots, held < slots + strata_total)
    live = jnp.sum(jnp.where(held, counts, 0.0), axis=1, keepdims=True)
    weight = lax.rsqrt(strata_total * jnp.maximum(counts, 1.0))
    picked = jnp.sum(dispatch[...] * raw, axis=1, keepdims=True)
    picked = picked * jnp.sum(member[...] * weight, axis=1, keepdims=True) * jnp.sqrt(live)
    examples = dispatch.shape[0]
    square = iota((examples, LANES), 0) == iota((examples, LANES), 1)
    out[...] = jnp.sum(jnp.where(square, picked, 0.0), axis=0)[:examples]


def shards(
    hidden,
    cotangent,
    adapter_down_weight,
    adapter_up_weight,
    width_projection_factor,
    rank_projection_factor,
    targets,
    strata,
    keep,
    shard_example_count,
    stratum_owner_table,
):
    examples = strata.shape[0]
    strata_total = stratum_owner_table.shape[0]
    owners, columns = lax.axis_size("dp"), lax.axis_size("x")
    slots = owners * CAP
    model, wide = width_projection_factor.shape
    rank, kr = rank_projection_factor.shape
    share = targets.shape[1]
    chips = owners * columns
    lanes = -(-(slots + strata_total) // LANES) * LANES

    payload, dispatch, member, notes = pl.pallas_call(
        project_kernel,
        out_shape=(
            jax.ShapeDtypeStruct((chips, CAP * PIECES, ROW), bf16),
            jax.ShapeDtypeStruct((examples, lanes), f32),
            jax.ShapeDtypeStruct((examples, lanes), f32),
            jax.ShapeDtypeStruct((8, lanes), f32),
        ),
        in_specs=[pl.BlockSpec(memory_space=pltpu.SMEM)] + [HBM] * 9,
        out_specs=(VMEM,) * 4,
        scratch_shapes=[
            pltpu.SMEM((examples,), i32),
            pltpu.SMEM((examples,), i32),
            pltpu.SMEM((strata_total,), i32),
            pltpu.SMEM((owners,), i32),
            pltpu.SMEM((slots + 1,), i32),
            pltpu.VMEM((2 * slots, SEQ, model), bf16),
            pltpu.VMEM((2 * rank, model), bf16),
            pltpu.VMEM((model, 2 * rank), bf16),
            pltpu.VMEM((model, wide), bf16),
            pltpu.VMEM((kr, rank), bf16),
            pltpu.VMEM((LANES, ROW), bf16),
            pltpu.SemaphoreType.DMA((3,)),
            pltpu.SemaphoreType.DMA((2 * slots,)),
            pltpu.SemaphoreType.DMA((7,)),
        ],
        compiler_params=pltpu.CompilerParams(vmem_limit_bytes=40 * 2**20),
        name="project",
    )(
        shard_example_count,
        *in_hbm(
            strata,
            keep,
            stratum_owner_table,
            hidden.reshape(examples, SEQ, model),
            cotangent.reshape(examples, SEQ, model),
            adapter_down_weight.T,
            adapter_up_weight,
            width_projection_factor,
            rank_projection_factor.T,
        )
    )
    payload, targets = lax.optimization_barrier((payload, targets))
    stacked, inverse = pl.pallas_call(
        target_kernel,
        out_shape=(
            jax.ShapeDtypeStruct((PIECES, share, ROW), bf16),
            jax.ShapeDtypeStruct((share, LANES), f32),
        ),
        in_specs=[pl.BlockSpec(memory_space=pl.ANY)],
        out_specs=(VMEM, VMEM),
        scratch_shapes=[pltpu.SemaphoreType.DMA((PIECES,))],
        compiler_params=pltpu.CompilerParams(vmem_limit_bytes=20 * 2**20),
        cost_estimate=pl.CostEstimate(flops=4 * share * FEAT, bytes_accessed=4 * share * FEAT, transcendentals=0),
        name="target_norms",
    )(targets)
    mine = lax.all_to_all(payload, ("x", "dp"), split_axis=0, concat_axis=0, tiled=True)
    other = lax.ppermute(mine, "core", [(n, (n + 1) % CORES) for n in range(CORES)])
    back = pl.pallas_call(
        score_kernel,
        out_shape=jax.ShapeDtypeStruct((chips * CORES, 1, lanes), f32),
        in_specs=[VMEM] * 5,
        out_specs=VMEM,
        compiler_params=pltpu.CompilerParams(vmem_limit_bytes=40 * 2**20),
        name="score",
    )(stacked, inverse, mine, other, notes)
    returned = lax.all_to_all(back, ("x", "dp", "core"), split_axis=0, concat_axis=0, tiled=True)
    return pl.pallas_call(
        functools.partial(finish_kernel, slots, strata_total),
        out_shape=jax.ShapeDtypeStruct((examples,), f32),
        in_specs=[VMEM] * 4,
        out_specs=VMEM,
        compiler_params=pltpu.CompilerParams(vmem_limit_bytes=4 * 2**20),
        name="finish",
    )(returned, dispatch, member, notes)


def solution(mesh):
    sizes = [mesh.shape[name] for name in ("groups", "dp", "tgt")]
    fine = jax.sharding.Mesh(
        mesh.devices.reshape(sizes[0], sizes[1], sizes[2] // CORES, CORES),
        ("groups", "dp", "x", "core"),
    )
    every = P(("groups", "dp", "x", "core"))
    whole = P()
    return jax.shard_map(
        shards,
        mesh=fine,
        in_specs=(
            every, every, whole, whole, whole, whole,
            P(("groups", "dp"), ("x", "core"), None),
            every, every, every, whole,
        ),
        out_specs=every,
        check_vma=False,
    )
```

```python
import functools
import math

import jax
import jax.numpy as jnp
from jax import lax
from jax.experimental import pallas as pl
from jax.experimental.pallas import tpu as pltpu
from jax.sharding import PartitionSpec as P

FEAT = 8192
CAP = 2
TGT = 768
TASKS = 16
SEQ = 8
CORES = 2
LANES = 128
ROW = 1024
PIECES = FEAT // ROW
GROUP = 8
epsilon = 1e-06
bf16, f32, i32 = jnp.bfloat16, jnp.float32, jnp.int32

HBM = pl.BlockSpec(memory_space=pltpu.HBM)
VMEM = pl.BlockSpec(memory_space=pltpu.VMEM)


def nn(a, b):
    return jnp.dot(a, b, preferred_element_type=f32)


def nt(a, b):
    return lax.dot_general(a, b, (((1,), (1,)), ((), ())), preferred_element_type=f32)


def in_hbm(*arrays):
    return [pltpu.with_memory_space_constraint(a, pltpu.HBM) for a in arrays]


def iota(shape, dim):
    return lax.broadcasted_iota(i32, shape, dim)


def project_kernel(
    place_of, present, strata, keep, table, hidden, cotangent, down_t, up, width, rank_t,
    payload, dispatch, member, notes,
    strata_s, keep_s, table_s, taken, chosen, x, adapters, adapters_t, width_v, rank_v, spread,
    small_sem, row_sem, weight_sem,
):
    examples, strata_total = strata_s.shape[0], table_s.shape[0]
    slots = x.shape[0] // 2
    owners = slots // CAP
    rank = down_t.shape[0]
    wide = width.shape[1]
    parts = 2
    early = 1
    depth = width.shape[0] // parts

    smalls = [
        pltpu.make_async_copy(a, b, small_sem.at[n])
        for n, (a, b) in enumerate(
            [(strata, strata_s), (keep, keep_s), (table, table_s)]
        )
    ]
    weights = [
        pltpu.make_async_copy(rank_t, rank_v, weight_sem.at[0]),
        pltpu.make_async_copy(down_t, adapters.at[pl.ds(0, rank)], weight_sem.at[1]),
        pltpu.make_async_copy(up, adapters.at[pl.ds(rank, rank)], weight_sem.at[2]),
    ] + [
        pltpu.make_async_copy(
            width.at[pl.ds(n * depth, depth)], width_v.at[pl.ds(n * depth, depth)], weight_sem.at[3 + n]
        )
        for n in range(parts)
    ]
    for copy in smalls + weights[: 3 + early]:
        copy.start()

    for n in range(owners):
        taken[n] = 0
    for n in range(slots + 1):
        chosen[n] = 0
    lane = iota((1, notes.shape[1]), 1)
    for copy in smalls:
        copy.wait()
    counts = jnp.zeros(lane.shape, f32)
    for e in range(examples):
        stratum = strata_s[e]
        live = jnp.where(jnp.logical_and(keep_s[e] == 1, e < present[0]), 1, 0)
        owner = table_s[stratum]
        place = taken[owner]
        taken[owner] = place + live
        slot = jnp.where(jnp.logical_and(live == 1, place < CAP), owner * CAP + place, slots)
        chosen[slot] = e
        counts += jnp.where(lane == slots + stratum, live.astype(f32), 0.0)
        member[e : e + 1, :] = (lane == slots + stratum).astype(f32)
        dispatch[e : e + 1, :] = jnp.where(jnp.logical_and(lane == slot, lane < slots), 1.0, 0.0)
    notes[...] = jnp.broadcast_to(counts, notes.shape)
    rows = []
    for n in range(slots):
        rows.append(pltpu.make_async_copy(hidden.at[chosen[n]], x.at[n], row_sem.at[n]))
        rows.append(
            pltpu.make_async_copy(cotangent.at[chosen[n]], x.at[slots + n], row_sem.at[slots + n])
        )
    for copy in rows + weights[3 + early :]:
        copy.start()

    half = PIECES // 2
    kr = rank_v.shape[0]
    per_row = ROW // wide
    tokens = GROUP * SEQ
    lines = GROUP * half
    spread[...] = (iota((LANES, ROW), 1) // kr == iota((LANES, ROW), 0)).astype(f32).astype(bf16)
    weights[0].wait()
    up_line = iota((per_row * lines, kr), 0)
    pick_up = (per_row * (up_line % half) + up_line // lines == iota((per_row * lines, kr), 1))
    rank_up_rows = nn(pick_up.astype(f32).astype(bf16), rank_v[...]).astype(bf16)
    pick_down = iota((kr * lines, kr), 0) // lines == iota((kr * lines, kr), 1)
    rank_down_rows = nn(pick_down.astype(f32).astype(bf16), rank_v[...]).astype(bf16)
    up_at, up_token = iota((per_row * lines, tokens), 0), iota((per_row * lines, tokens), 1)
    up_mask = (up_at % lines) // half == up_token // SEQ
    down_at, down_token = iota((kr * lines, half * tokens), 0), iota((kr * lines, half * tokens), 1)
    down_mask = jnp.logical_and(
        (down_at % lines) // half == (down_token % tokens) // SEQ, down_at % half == down_token // tokens
    )
    rank_at = iota((lines, ROW), 1) % kr
    for copy in weights[1:3]:
        copy.wait()
    adapters_t[...] = adapters[...].T
    for copy in rows:
        copy.wait()

    for g in range(slots // GROUP):
        model = x.shape[2]
        def both(lo, size):
            return jnp.concatenate(
                [
                    x[g * GROUP : (g + 1) * GROUP, :, lo : lo + size].reshape(tokens, size),
                    x[slots + g * GROUP : slots + (g + 1) * GROUP, :, lo : lo + size].reshape(tokens, size),
                ],
                axis=0,
            )

        adapted = nn(both(0, model), adapters_t[...])
        down_act = adapted[:tokens, :rank].astype(bf16)
        up_back = adapted[tokens:, rank:].astype(bf16)
        left_up = jnp.where(up_mask, nt(rank_up_rows, down_act), 0.0).astype(bf16)
        left_down = nt(rank_down_rows, jnp.concatenate([up_back] * half, axis=0))
        left_down = jnp.where(down_mask, left_down, 0.0).astype(bf16)
        for n in range(parts):
            if g == 0:
                weights[3 + n].wait()
            span = pl.ds(n * depth, depth)
            part = nn(both(n * depth, depth), width_v[span, :])
            projected = part if n == 0 else projected + part
        wide_hidden = projected[:tokens].astype(bf16)
        wide_back = projected[tokens:].astype(bf16)
        stacked = jnp.concatenate(
            [wide_hidden[:, n * LANES : (n + 1) * LANES] for n in range(half)], axis=0
        )
        down_grad = nn(left_down, stacked).astype(bf16)
        up_grad = nn(left_up, wide_back)
        up_rows = jnp.concatenate(
            [up_grad[n * lines : (n + 1) * lines] for n in range(per_row)], axis=1
        )
        repeated = nn(down_grad, spread[...])
        down_rows = repeated[:lines]
        for n in range(1, kr):
            down_rows = jnp.where(rank_at == n, repeated[n * lines : (n + 1) * lines], down_rows)

        per_owner = CAP * half
        for n in range(GROUP // CAP):
            owner = g * (GROUP // CAP) + n
            piece = jnp.concatenate(
                [
                    up_rows[n * per_owner : (n + 1) * per_owner],
                    down_rows[n * per_owner : (n + 1) * per_owner],
                ],
                axis=0,
            ).astype(bf16)
            for at in place_of(owner):
                payload[at] = piece


def norm_kernel(slots, direct, targets, payload, stacked, inverse, row_inverse, sem):
    copies = [
        pltpu.make_async_copy(
            targets.at[0, :, pl.ds(n * ROW, ROW)], stacked.at[n], sem.at[n]
        )
        for n in range(PIECES)
    ]
    for copy in copies:
        copy.start()
    total = jnp.zeros((targets.shape[1], LANES), f32)
    for n in range(PIECES):
        copies[n].wait()
        for m in range(ROW // LANES):
            part = stacked[n, :, m * LANES : (m + 1) * LANES].astype(f32)
            total += part * part
    scale = math.sqrt(FEAT) / (TGT // TASKS)
    inverse[...] = jnp.broadcast_to(
        scale * lax.rsqrt(jnp.sum(total, axis=1, keepdims=True) + epsilon), inverse.shape
    )
    owners, pieces = slots // CAP, payload.shape[1]
    step = payload.shape[0] // owners
    values = jnp.concatenate([payload[n * step] for n in range(owners)], axis=0).astype(f32)
    squares = jnp.sum(values * values, axis=1, keepdims=True)
    at = (owners * pieces, row_inverse.shape[1])
    line = iota(at, 0)
    owner = line // pieces
    if direct:
        owner = jnp.bitwise_xor(owner, lax.axis_index("dp"))
    slot = owner * CAP + line % pieces % (pieces // 2) // (PIECES // 2)
    squares = jnp.sum(jnp.where(slot == iota(at, 1), squares, 0.0), axis=0, keepdims=True)
    row_inverse[...] = jnp.broadcast_to(lax.rsqrt(squares + epsilon), row_inverse.shape)


def direct_groups(payload, other, *arrived):
    d, x, core = (lax.axis_index(name) for name in ("dp", "x", "core"))
    columns = lax.axis_size("x")

    def place(k, across, on):
        return (jnp.bitwise_xor(d, k) * columns + jnp.bitwise_xor(x, across)) * CORES + on

    pieces = CAP * PIECES
    groups = [(payload[0], place(0, 0, core)), (other[0], place(0, 0, 1 - core))]
    arrived, from_core = arrived[:-1], arrived[-1]
    for on, mine in ((core, True), (1 - core, False)):
        start = 0
        for k, ref in zip(direct_order(lax.axis_size("dp")), arrived):
            span = ref.shape[0]
            rows = ref[...] if mine else from_core[start : start + span]
            start += span
            if k == 0:
                groups.append((rows, place(0, 1, on)))
            else:
                groups.append((rows[:pieces], place(k, on, on)))
                groups.append((rows[pieces:], place(k, on, 1 - on)))
    return groups


def gathered_groups(mine, other):
    core = lax.axis_index("core")
    sources = mine.shape[0]
    groups = []
    step = LANES // (CAP * PIECES)
    for b in range(0, sources, step):
        groups += [(mine[n], n * CORES + core) for n in range(b, b + step)]
        groups += [(other[n], n * CORES + 1 - core) for n in range(b, b + step)]
    return groups


def score_kernel(groups_of, stacked, inverse, notes, *refs):
    back = refs[-1]
    per_task = TGT // TASKS
    half = PIECES // 2
    first = lax.axis_index("dp") * CAP
    share = stacked.shape[1]
    line = iota((1, CORES * LANES), 1)
    piece_of = (line // (CAP * half)) % 2 * half + line % half
    inv = inverse[...]
    pieces = CAP * PIECES
    per_block = CORES * LANES // pieces
    source = iota((per_block, LANES), 0)
    lane = iota((per_block, LANES), 1)
    groups = groups_of(*refs[:-1])
    for b in range(0, len(groups), per_block):
        block = jnp.concatenate([rows for rows, _ in groups[b : b + per_block]], axis=0)
        whole = nt(stacked[...].reshape(PIECES * share, ROW), block)
        products = whole[:share]
        for n in range(1, PIECES):
            products = jnp.where(piece_of == n, whole[n * share : (n + 1) * share], products)
        best = []
        for c in range(CORES):
            total = products[:, c * LANES : (c + 1) * LANES]
            for shift in (1, 2, CAP * half):
                total = total + pltpu.roll(total, LANES - shift, 1)
            total = jnp.maximum(total, 0.0) * inv
            top = jnp.sum(total[:per_task], axis=0, keepdims=True)
            for n in range(1, share // per_task):
                top = jnp.maximum(
                    top, jnp.sum(total[n * per_task : (n + 1) * per_task], axis=0, keepdims=True)
                )
            best.append(top)
        table = jnp.where(source < per_block // CORES, best[0], best[1])
        scores = jnp.broadcast_to(notes[0:1, :], (per_block, notes.shape[1]))
        for n in range(CAP):
            at = lane == source % (per_block // CORES) * pieces + n * half
            column = jnp.sum(jnp.where(at, table, 0.0), axis=1, keepdims=True)
            scores = jnp.where(iota(scores.shape, 1) == first + n, column, scores)
        for n in range(per_block):
            back[groups[b + n][1]] = scores[n : n + 1]


def finish_kernel(slots, strata_total, returned, dispatch, member, row_inverse, out):
    values = returned[:, 0, :]
    raw = jnp.max(values, axis=0, keepdims=True) * row_inverse[0:1, :]
    counts = jnp.sum(values, axis=0, keepdims=True)
    held = iota(counts.shape, 1)
    held = jnp.logical_and(held >= slots, held < slots + strata_total)
    live = jnp.sum(jnp.where(held, counts, 0.0), axis=1, keepdims=True)
    weight = lax.rsqrt(strata_total * jnp.maximum(counts, 1.0))
    picked = jnp.sum(dispatch[...] * raw, axis=1, keepdims=True)
    picked = picked * jnp.sum(member[...] * weight, axis=1, keepdims=True) * jnp.sqrt(live)
    examples = dispatch.shape[0]
    square = iota((examples, LANES), 0) == iota((examples, LANES), 1)
    out[...] = jnp.sum(jnp.where(square, picked, 0.0), axis=0)[:examples]


def direct_order(owners):
    return list(range(owners - 1, -1, -1))


def direct_rows(payload, owners, columns):
    swap = [(n, n ^ 1) for n in range(CORES)]
    other = lax.ppermute(payload, "core", swap)
    arrived = []
    for k in direct_order(owners):
        pairs = []
        for d in range(owners):
            for x in range(columns):
                for c in range(CORES):
                    to = (d ^ k, x ^ (1 if k == 0 else c), c)
                    pairs.append(
                        ((d * columns + x) * CORES + c, (to[0] * columns + to[1]) * CORES + to[2])
                    )
        rows = payload[0] if k == 0 else jnp.concatenate([payload[k], other[k]], axis=0)
        arrived.append(lax.ppermute(rows, ("dp", "x", "core"), pairs))
    from_core = lax.ppermute(jnp.concatenate(arrived, axis=0), "core", swap)
    return [payload, other] + arrived + [from_core]


def shards(
    hidden,
    cotangent,
    adapter_down_weight,
    adapter_up_weight,
    width_projection_factor,
    rank_projection_factor,
    targets,
    strata,
    keep,
    shard_example_count,
    stratum_owner_table,
):
    examples = strata.shape[0]
    strata_total = stratum_owner_table.shape[0]
    owners, columns = lax.axis_size("dp"), lax.axis_size("x")
    slots = owners * CAP
    model, wide = width_projection_factor.shape
    rank, kr = rank_projection_factor.shape
    share = targets.shape[1]
    chips = owners * columns
    direct = columns == 2 and owners in (2, 4)

    def places(owner):
        if direct:
            return [jnp.bitwise_xor(lax.axis_index("dp"), owner)]
        return [owner * columns + n for n in range(columns)]

    lanes = -(-(slots + strata_total) // LANES) * LANES

    payload, dispatch, member, notes = pl.pallas_call(
        functools.partial(project_kernel, places),
        out_shape=(
            jax.ShapeDtypeStruct((owners if direct else chips, CAP * PIECES, ROW), bf16),
            jax.ShapeDtypeStruct((examples, lanes), f32),
            jax.ShapeDtypeStruct((examples, lanes), f32),
            jax.ShapeDtypeStruct((8, lanes), f32),
        ),
        in_specs=[pl.BlockSpec(memory_space=pltpu.SMEM)] + [HBM] * 9,
        out_specs=(VMEM,) * 4,
        scratch_shapes=[
            pltpu.SMEM((examples,), i32),
            pltpu.SMEM((examples,), i32),
            pltpu.SMEM((strata_total,), i32),
            pltpu.SMEM((owners,), i32),
            pltpu.SMEM((slots + 1,), i32),
            pltpu.VMEM((2 * slots, SEQ, model), bf16),
            pltpu.VMEM((2 * rank, model), bf16),
            pltpu.VMEM((model, 2 * rank), bf16),
            pltpu.VMEM((model, wide), bf16),
            pltpu.VMEM((kr, rank), bf16),
            pltpu.VMEM((LANES, ROW), bf16),
            pltpu.SemaphoreType.DMA((3,)),
            pltpu.SemaphoreType.DMA((2 * slots,)),
            pltpu.SemaphoreType.DMA((7,)),
        ],
        compiler_params=pltpu.CompilerParams(vmem_limit_bytes=40 * 2**20),
        name="project",
    )(
        shard_example_count,
        *in_hbm(
            strata,
            keep,
            stratum_owner_table,
            hidden.reshape(examples, SEQ, model),
            cotangent.reshape(examples, SEQ, model),
            adapter_down_weight.T,
            adapter_up_weight,
            width_projection_factor,
            rank_projection_factor.T,
        )
    )
    stacked, inverse, row_inverse = pl.pallas_call(
        functools.partial(norm_kernel, slots, direct),
        out_shape=(
            jax.ShapeDtypeStruct((PIECES, share, ROW), bf16),
            jax.ShapeDtypeStruct((share, LANES), f32),
            jax.ShapeDtypeStruct((8, lanes), f32),
        ),
        in_specs=[pl.BlockSpec(memory_space=pl.ANY), VMEM],
        out_specs=(VMEM, VMEM, VMEM),
        scratch_shapes=[pltpu.SemaphoreType.DMA((PIECES,))],
        compiler_params=pltpu.CompilerParams(vmem_limit_bytes=20 * 2**20),
        cost_estimate=pl.CostEstimate(flops=4 * share * FEAT, bytes_accessed=4 * share * FEAT, transcendentals=0),
        name="norms",
    )(targets, payload)
    if direct:
        rows = direct_rows(payload, owners, columns)
    else:
        mine = lax.all_to_all(payload, ("dp", "x"), split_axis=0, concat_axis=0, tiled=True)
        rows = [mine, lax.ppermute(mine, "core", [(n, n ^ 1) for n in range(CORES)])]
    back = pl.pallas_call(
        functools.partial(score_kernel, direct_groups if direct else gathered_groups),
        out_shape=jax.ShapeDtypeStruct((chips * CORES, 1, lanes), f32),
        in_specs=[VMEM] * (3 + len(rows)),
        out_specs=VMEM,
        compiler_params=pltpu.CompilerParams(vmem_limit_bytes=40 * 2**20),
        name="score",
    )(stacked, inverse, notes, *rows)
    returned = lax.all_to_all(back, ("dp", "x", "core"), split_axis=0, concat_axis=0, tiled=True)
    return pl.pallas_call(
        functools.partial(finish_kernel, slots, strata_total),
        out_shape=jax.ShapeDtypeStruct((examples,), f32),
        in_specs=[VMEM] * 4,
        out_specs=VMEM,
        compiler_params=pltpu.CompilerParams(vmem_limit_bytes=4 * 2**20),
        name="finish",
    )(returned, dispatch, member, row_inverse)


def solution(mesh):
    sizes = [mesh.shape[name] for name in ("groups", "dp", "tgt")]
    fine = jax.sharding.Mesh(
        mesh.devices.reshape(sizes[0], sizes[1], sizes[2] // CORES, CORES),
        ("groups", "dp", "x", "core"),
    )
    every = P(("groups", "dp", "x", "core"))
    whole = P()
    return jax.shard_map(
        shards,
        mesh=fine,
        in_specs=(
            every, every, whole, whole, whole, whole,
            P(("groups", "dp"), ("x", "core"), None),
            every, every, every, whole,
        ),
        out_specs=every,
        check_vma=False,
    )
```

```python
import functools
import math

import jax
import jax.numpy as jnp
from jax import lax
from jax.experimental import pallas as pl
from jax.experimental.pallas import tpu as pltpu
from jax.sharding import PartitionSpec as P

FEAT = 8192
CAP = 2
TGT = 768
TASKS = 16
SEQ = 8
CORES = 2
LANES = 128
ROW = 1024
PIECES = FEAT // ROW
GROUP = 8
epsilon = 1e-06
bf16, f32, i32 = jnp.bfloat16, jnp.float32, jnp.int32

HBM = pl.BlockSpec(memory_space=pltpu.HBM)
VMEM = pl.BlockSpec(memory_space=pltpu.VMEM)


def nn(a, b):
    return jnp.dot(a, b, preferred_element_type=f32)


def nt(a, b):
    return lax.dot_general(a, b, (((1,), (1,)), ((), ())), preferred_element_type=f32)


def in_hbm(*arrays):
    return [pltpu.with_memory_space_constraint(a, pltpu.HBM) for a in arrays]


def iota(shape, dim):
    return lax.broadcasted_iota(i32, shape, dim)


def project_kernel(
    place_of, strata, keep, table, hidden, cotangent, down_t, up, width, rank_t,
    payload, dispatch, member,
    strata_s, keep_s, table_s, taken, chosen, x, adapters, adapters_t, width_v, rank_v, spread,
    small_sem, row_sem, weight_sem,
):
    examples, strata_total = strata_s.shape[0], table_s.shape[0]
    slots = x.shape[0] // 2
    owners = slots // CAP
    rank = down_t.shape[0]
    wide = width.shape[1]
    parts = 2
    early = 1
    depth = width.shape[0] // parts

    smalls = [
        pltpu.make_async_copy(a, b, small_sem.at[n])
        for n, (a, b) in enumerate(
            [(strata, strata_s), (keep, keep_s), (table, table_s)]
        )
    ]
    weights = [
        pltpu.make_async_copy(rank_t, rank_v, weight_sem.at[0]),
        pltpu.make_async_copy(down_t, adapters.at[pl.ds(0, rank)], weight_sem.at[1]),
        pltpu.make_async_copy(up, adapters.at[pl.ds(rank, rank)], weight_sem.at[2]),
    ] + [
        pltpu.make_async_copy(
            width.at[pl.ds(n * depth, depth)], width_v.at[pl.ds(n * depth, depth)], weight_sem.at[3 + n]
        )
        for n in range(parts)
    ]
    for copy in smalls + weights[: 3 + early]:
        copy.start()

    for n in range(owners):
        taken[n] = 0
    for n in range(slots + 1):
        chosen[n] = 0
    lane = iota((1, member.shape[1]), 1)
    for copy in smalls:
        copy.wait()
    for e in range(examples):
        stratum = strata_s[e]
        live = jnp.where(keep_s[e] == 1, 1, 0)
        owner = table_s[stratum]
        place = taken[owner]
        taken[owner] = place + live
        slot = jnp.where(jnp.logical_and(live == 1, place < CAP), owner * CAP + place, slots)
        chosen[slot] = e
        member[e : e + 1, :] = jnp.where(lane == slots + stratum, live.astype(f32), 0.0)
        dispatch[e : e + 1, :] = jnp.where(jnp.logical_and(lane == slot, lane < slots), 1.0, 0.0)
    rows = []
    for n in range(slots):
        rows.append(pltpu.make_async_copy(hidden.at[chosen[n]], x.at[n], row_sem.at[n]))
        rows.append(
            pltpu.make_async_copy(cotangent.at[chosen[n]], x.at[slots + n], row_sem.at[slots + n])
        )
    for copy in rows + weights[3 + early :]:
        copy.start()

    half = PIECES // 2
    kr = rank_v.shape[0]
    per_row = ROW // wide
    tokens = GROUP * SEQ
    lines = GROUP * half
    spread[...] = (iota((LANES, ROW), 1) // kr == iota((LANES, ROW), 0)).astype(f32).astype(bf16)
    weights[0].wait()
    up_line = iota((per_row * lines, kr), 0)
    pick_up = (per_row * (up_line % half) + up_line // lines == iota((per_row * lines, kr), 1))
    rank_up_rows = nn(pick_up.astype(f32).astype(bf16), rank_v[...]).astype(bf16)
    pick_down = iota((kr * lines, kr), 0) // lines == iota((kr * lines, kr), 1)
    rank_down_rows = nn(pick_down.astype(f32).astype(bf16), rank_v[...]).astype(bf16)
    up_at, up_token = iota((per_row * lines, tokens), 0), iota((per_row * lines, tokens), 1)
    up_mask = (up_at % lines) // half == up_token // SEQ
    down_at, down_token = iota((kr * lines, half * tokens), 0), iota((kr * lines, half * tokens), 1)
    down_mask = jnp.logical_and(
        (down_at % lines) // half == (down_token % tokens) // SEQ, down_at % half == down_token // tokens
    )
    rank_at = iota((lines, ROW), 1) % kr
    for copy in weights[1:3]:
        copy.wait()
    adapters_t[...] = adapters[...].T
    for copy in rows:
        copy.wait()

    for g in range(slots // GROUP):
        model = x.shape[2]
        def both(lo, size):
            return jnp.concatenate(
                [
                    x[g * GROUP : (g + 1) * GROUP, :, lo : lo + size].reshape(tokens, size),
                    x[slots + g * GROUP : slots + (g + 1) * GROUP, :, lo : lo + size].reshape(tokens, size),
                ],
                axis=0,
            )

        adapted = nn(both(0, model), adapters_t[...])
        down_act = adapted[:tokens, :rank].astype(bf16)
        up_back = adapted[tokens:, rank:].astype(bf16)
        left_up = jnp.where(up_mask, nt(rank_up_rows, down_act), 0.0).astype(bf16)
        left_down = nt(rank_down_rows, jnp.concatenate([up_back] * half, axis=0))
        left_down = jnp.where(down_mask, left_down, 0.0).astype(bf16)
        for n in range(parts):
            if g == 0:
                weights[3 + n].wait()
            span = pl.ds(n * depth, depth)
            part = nn(both(n * depth, depth), width_v[span, :])
            projected = part if n == 0 else projected + part
        wide_hidden = projected[:tokens].astype(bf16)
        wide_back = projected[tokens:].astype(bf16)
        stacked = jnp.concatenate(
            [wide_hidden[:, n * LANES : (n + 1) * LANES] for n in range(half)], axis=0
        )
        down_grad = nn(left_down, stacked).astype(bf16)
        up_grad = nn(left_up, wide_back)
        up_rows = jnp.concatenate(
            [up_grad[n * lines : (n + 1) * lines] for n in range(per_row)], axis=1
        )
        repeated = nn(down_grad, spread[...])
        down_rows = repeated[:lines]
        for n in range(1, kr):
            down_rows = jnp.where(rank_at == n, repeated[n * lines : (n + 1) * lines], down_rows)

        per_owner = CAP * half
        for n in range(GROUP // CAP):
            owner = g * (GROUP // CAP) + n
            piece = jnp.concatenate(
                [
                    up_rows[n * per_owner : (n + 1) * per_owner],
                    down_rows[n * per_owner : (n + 1) * per_owner],
                ],
                axis=0,
            ).astype(bf16)
            for at in place_of(owner):
                payload[at] = piece


def norm_kernel(
    slots, direct, present, targets, payload, dispatch, member,
    stacked, inverse, picks, counts, sem,
):
    copies = [
        pltpu.make_async_copy(
            targets.at[0, :, pl.ds(n * ROW, ROW)], stacked.at[n], sem.at[n]
        )
        for n in range(PIECES)
    ]
    for copy in copies:
        copy.start()
    total = jnp.zeros((targets.shape[1], LANES), f32)
    for n in range(PIECES):
        copies[n].wait()
        for m in range(ROW // LANES):
            part = stacked[n, :, m * LANES : (m + 1) * LANES].astype(f32)
            total += part * part
    scale = math.sqrt(FEAT) / (TGT // TASKS)
    inverse[...] = jnp.broadcast_to(
        scale * lax.rsqrt(jnp.sum(total, axis=1, keepdims=True) + epsilon), inverse.shape
    )
    owners, pieces = slots // CAP, payload.shape[1]
    step = payload.shape[0] // owners
    values = jnp.concatenate([payload[n * step] for n in range(owners)], axis=0).astype(f32)
    squares = jnp.sum(values * values, axis=1, keepdims=True)
    at = (owners * pieces, picks.shape[1])
    line = iota(at, 0)
    owner = line // pieces
    if direct:
        owner = jnp.bitwise_xor(owner, lax.axis_index("dp"))
    slot = owner * CAP + line % pieces % (pieces // 2) // (PIECES // 2)
    squares = jnp.sum(jnp.where(slot == iota(at, 1), squares, 0.0), axis=0, keepdims=True)
    used = iota(picks.shape, 0) < present[0]
    picks[...] = jnp.where(used, dispatch[...] * lax.rsqrt(squares + epsilon), 0.0)
    held = jnp.sum(jnp.where(used, member[...], 0.0), axis=0, keepdims=True)
    counts[...] = jnp.broadcast_to(held, counts.shape)


def direct_groups(payload, other, *arrived):
    d, x, core = (lax.axis_index(name) for name in ("dp", "x", "core"))
    columns = lax.axis_size("x")

    def place(k, across, on):
        return (jnp.bitwise_xor(d, k) * columns + jnp.bitwise_xor(x, across)) * CORES + on

    pieces = CAP * PIECES
    groups = [(payload[0], place(0, 0, core)), (other[0], place(0, 0, 1 - core))]
    arrived, from_core = arrived[:-1], arrived[-1]
    for on, mine in ((core, True), (1 - core, False)):
        start = 0
        for k, ref in zip(direct_order(lax.axis_size("dp")), arrived):
            span = ref.shape[0]
            rows = ref[...] if mine else from_core[start : start + span]
            start += span
            if k == 0:
                groups.append((rows, place(0, 1, on)))
            else:
                groups.append((rows[:pieces], place(k, on, on)))
                groups.append((rows[pieces:], place(k, on, 1 - on)))
    return groups


def gathered_groups(mine, other):
    core = lax.axis_index("core")
    sources = mine.shape[0]
    groups = []
    step = LANES // (CAP * PIECES)
    for b in range(0, sources, step):
        groups += [(mine[n], n * CORES + core) for n in range(b, b + step)]
        groups += [(other[n], n * CORES + 1 - core) for n in range(b, b + step)]
    return groups


def score_kernel(groups_of, stacked, inverse, counts, *refs):
    back = refs[-1]
    per_task = TGT // TASKS
    half = PIECES // 2
    first = lax.axis_index("dp") * CAP
    share = stacked.shape[1]
    line = iota((1, CORES * LANES), 1)
    piece_of = (line // (CAP * half)) % 2 * half + line % half
    inv = inverse[...]
    pieces = CAP * PIECES
    per_block = CORES * LANES // pieces
    source = iota((per_block, LANES), 0)
    lane = iota((per_block, LANES), 1)
    groups = groups_of(*refs[:-1])
    for b in range(0, len(groups), per_block):
        block = jnp.concatenate([rows for rows, _ in groups[b : b + per_block]], axis=0)
        whole = nt(stacked[...].reshape(PIECES * share, ROW), block)
        products = whole[:share]
        for n in range(1, PIECES):
            products = jnp.where(piece_of == n, whole[n * share : (n + 1) * share], products)
        best = []
        for c in range(CORES):
            total = products[:, c * LANES : (c + 1) * LANES]
            for shift in (1, 2, CAP * half):
                total = total + pltpu.roll(total, LANES - shift, 1)
            total = jnp.maximum(total, 0.0) * inv
            top = jnp.sum(total[:per_task], axis=0, keepdims=True)
            for n in range(1, share // per_task):
                top = jnp.maximum(
                    top, jnp.sum(total[n * per_task : (n + 1) * per_task], axis=0, keepdims=True)
                )
            best.append(top)
        table = jnp.where(source < per_block // CORES, best[0], best[1])
        scores = jnp.broadcast_to(counts[0:1, :], (per_block, counts.shape[1]))
        for n in range(CAP):
            at = lane == source % (per_block // CORES) * pieces + n * half
            column = jnp.sum(jnp.where(at, table, 0.0), axis=1, keepdims=True)
            scores = jnp.where(iota(scores.shape, 1) == first + n, column, scores)
        for n in range(per_block):
            back[groups[b + n][1]] = scores[n : n + 1]


def finish_kernel(slots, strata_total, returned, picks, member, out):
    values = returned[:, 0, :]
    raw = jnp.max(values, axis=0, keepdims=True)
    counts = jnp.sum(values, axis=0, keepdims=True)
    held = iota(counts.shape, 1)
    held = jnp.logical_and(held >= slots, held < slots + strata_total)
    live = jnp.sum(jnp.where(held, counts, 0.0), axis=1, keepdims=True)
    weight = lax.rsqrt(strata_total * jnp.maximum(counts, 1.0))
    picked = jnp.sum(picks[...] * raw, axis=1, keepdims=True)
    picked = picked * jnp.sum(member[...] * weight, axis=1, keepdims=True) * jnp.sqrt(live)
    examples = picks.shape[0]
    square = iota((examples, LANES), 0) == iota((examples, LANES), 1)
    out[...] = jnp.sum(jnp.where(square, picked, 0.0), axis=0)[:examples]


def direct_order(owners):
    return [2, 1, 3, 0] if owners == 4 else [1, 0]


def direct_rows(payload, owners, columns, norms):
    swap = [(n, n ^ 1) for n in range(CORES)]
    other = lax.ppermute(payload, "core", swap)
    arrived = []
    for k in direct_order(owners):
        pairs = []
        for d in range(owners):
            for x in range(columns):
                for c in range(CORES):
                    to = (d ^ k, x ^ (1 if k == 0 else c), c)
                    pairs.append(
                        ((d * columns + x) * CORES + c, (to[0] * columns + to[1]) * CORES + to[2])
                    )
        rows = payload[0] if k == 0 else jnp.concatenate([payload[k], other[k]], axis=0)
        arrived.append(lax.ppermute(rows, ("dp", "x", "core"), pairs))
    arrived, norms = lax.optimization_barrier((arrived, norms))
    from_core = lax.ppermute(jnp.concatenate(arrived, axis=0), "core", swap)
    return [payload, other] + arrived + [from_core], norms


def shards(
    hidden,
    cotangent,
    adapter_down_weight,
    adapter_up_weight,
    width_projection_factor,
    rank_projection_factor,
    targets,
    strata,
    keep,
    shard_example_count,
    stratum_owner_table,
):
    examples = strata.shape[0]
    strata_total = stratum_owner_table.shape[0]
    owners, columns = lax.axis_size("dp"), lax.axis_size("x")
    slots = owners * CAP
    model, wide = width_projection_factor.shape
    rank, kr = rank_projection_factor.shape
    share = targets.shape[1]
    chips = owners * columns
    direct = columns == 2 and owners in (2, 4)

    def places(owner):
        if direct:
            return [jnp.bitwise_xor(lax.axis_index("dp"), owner)]
        return [owner * columns + n for n in range(columns)]

    lanes = -(-(slots + strata_total) // LANES) * LANES

    payload, dispatch, member = pl.pallas_call(
        functools.partial(project_kernel, places),
        out_shape=(
            jax.ShapeDtypeStruct((owners if direct else chips, CAP * PIECES, ROW), bf16),
            jax.ShapeDtypeStruct((examples, lanes), f32),
            jax.ShapeDtypeStruct((examples, lanes), f32),
        ),
        in_specs=[HBM] * 9,
        out_specs=(VMEM,) * 3,
        scratch_shapes=[
            pltpu.SMEM((examples,), i32),
            pltpu.SMEM((examples,), i32),
            pltpu.SMEM((strata_total,), i32),
            pltpu.SMEM((owners,), i32),
            pltpu.SMEM((slots + 1,), i32),
            pltpu.VMEM((2 * slots, SEQ, model), bf16),
            pltpu.VMEM((2 * rank, model), bf16),
            pltpu.VMEM((model, 2 * rank), bf16),
            pltpu.VMEM((model, wide), bf16),
            pltpu.VMEM((kr, rank), bf16),
            pltpu.VMEM((LANES, ROW), bf16),
            pltpu.SemaphoreType.DMA((3,)),
            pltpu.SemaphoreType.DMA((2 * slots,)),
            pltpu.SemaphoreType.DMA((7,)),
        ],
        compiler_params=pltpu.CompilerParams(vmem_limit_bytes=40 * 2**20),
        name="project",
    )(
        *in_hbm(
            strata,
            keep,
            stratum_owner_table,
            hidden.reshape(examples, SEQ, model),
            cotangent.reshape(examples, SEQ, model),
            adapter_down_weight.T,
            adapter_up_weight,
            width_projection_factor,
            rank_projection_factor.T,
        )
    )
    stacked, inverse, picks, counts = pl.pallas_call(
        functools.partial(norm_kernel, slots, direct),
        out_shape=(
            jax.ShapeDtypeStruct((PIECES, share, ROW), bf16),
            jax.ShapeDtypeStruct((share, LANES), f32),
            jax.ShapeDtypeStruct((examples, lanes), f32),
            jax.ShapeDtypeStruct((8, lanes), f32),
        ),
        in_specs=[
            pl.BlockSpec(memory_space=pltpu.SMEM), pl.BlockSpec(memory_space=pl.ANY), VMEM, VMEM, VMEM
        ],
        out_specs=(VMEM,) * 4,
        scratch_shapes=[pltpu.SemaphoreType.DMA((PIECES,))],
        compiler_params=pltpu.CompilerParams(vmem_limit_bytes=20 * 2**20),
        cost_estimate=pl.CostEstimate(flops=4 * share * FEAT, bytes_accessed=4 * share * FEAT, transcendentals=0),
        name="norms",
    )(shard_example_count, targets, payload, dispatch, member)
    if direct:
        rows, (stacked, inverse, picks, counts) = direct_rows(payload, owners, columns, (stacked, inverse, picks, counts))
    else:
        mine = lax.all_to_all(payload, ("dp", "x"), split_axis=0, concat_axis=0, tiled=True)
        rows = [mine, lax.ppermute(mine, "core", [(n, n ^ 1) for n in range(CORES)])]
    back = pl.pallas_call(
        functools.partial(score_kernel, direct_groups if direct else gathered_groups),
        out_shape=jax.ShapeDtypeStruct((chips * CORES, 1, lanes), f32),
        in_specs=[VMEM] * (3 + len(rows)),
        out_specs=VMEM,
        compiler_params=pltpu.CompilerParams(vmem_limit_bytes=40 * 2**20),
        name="score",
    )(stacked, inverse, counts, *rows)
    returned = lax.all_to_all(back, ("dp", "x", "core"), split_axis=0, concat_axis=0, tiled=True)
    return pl.pallas_call(
        functools.partial(finish_kernel, slots, strata_total),
        out_shape=jax.ShapeDtypeStruct((examples,), f32),
        in_specs=[VMEM] * 3,
        out_specs=VMEM,
        compiler_params=pltpu.CompilerParams(vmem_limit_bytes=4 * 2**20),
        name="finish",
    )(returned, picks, member)


def solution(mesh):
    sizes = [mesh.shape[name] for name in ("groups", "dp", "tgt")]
    fine = jax.sharding.Mesh(
        mesh.devices.reshape(sizes[0], sizes[1], sizes[2] // CORES, CORES),
        ("groups", "dp", "x", "core"),
    )
    every = P(("groups", "dp", "x", "core"))
    whole = P()
    return jax.shard_map(
        shards,
        mesh=fine,
        in_specs=(
            every, every, whole, whole, whole, whole,
            P(("groups", "dp"), ("x", "core"), None),
            every, every, every, whole,
        ),
        out_specs=every,
        check_vma=False,
    )
```

```python
import functools
import math

import jax
import jax.numpy as jnp
from jax import lax
from jax.experimental import pallas as pl
from jax.experimental.pallas import tpu as pltpu
from jax.sharding import PartitionSpec as P

FEAT = 8192
CAP = 2
TGT = 768
TASKS = 16
SEQ = 8
CORES = 2
LANES = 128
ROW = 1024
PIECES = FEAT // ROW
GROUP = 8
epsilon = 1e-06
bf16, f32, i32 = jnp.bfloat16, jnp.float32, jnp.int32

HBM = pl.BlockSpec(memory_space=pltpu.HBM)
VMEM = pl.BlockSpec(memory_space=pltpu.VMEM)


def nn(a, b):
    return jnp.dot(a, b, preferred_element_type=f32)


def nt(a, b):
    return lax.dot_general(a, b, (((1,), (1,)), ((), ())), preferred_element_type=f32)


def in_hbm(*arrays):
    return [pltpu.with_memory_space_constraint(a, pltpu.HBM) for a in arrays]


def iota(shape, dim):
    return lax.broadcasted_iota(i32, shape, dim)


def project_kernel(
    place_of, strata, keep, table, hidden, cotangent, down_t, up, width, rank_t,
    payload, dispatch, member,
    strata_s, keep_s, table_s, taken, chosen, x, adapters, adapters_t, width_v, rank_v, spread,
    small_sem, row_sem, weight_sem,
):
    examples, strata_total = strata_s.shape[0], table_s.shape[0]
    slots = x.shape[0] // 2
    owners = slots // CAP
    rank = down_t.shape[0]
    wide = width.shape[1]
    parts = 2
    early = 1
    depth = width.shape[0] // parts

    smalls = [
        pltpu.make_async_copy(a, b, small_sem.at[n])
        for n, (a, b) in enumerate(
            [(strata, strata_s), (keep, keep_s), (table, table_s)]
        )
    ]
    weights = [
        pltpu.make_async_copy(rank_t, rank_v, weight_sem.at[0]),
        pltpu.make_async_copy(down_t, adapters.at[pl.ds(0, rank)], weight_sem.at[1]),
        pltpu.make_async_copy(up, adapters.at[pl.ds(rank, rank)], weight_sem.at[2]),
    ] + [
        pltpu.make_async_copy(
            width.at[pl.ds(n * depth, depth)], width_v.at[pl.ds(n * depth, depth)], weight_sem.at[3 + n]
        )
        for n in range(parts)
    ]
    for copy in smalls + weights[: 3 + early]:
        copy.start()

    for n in range(owners):
        taken[n] = 0
    for n in range(slots + 1):
        chosen[n] = 0
    lane = iota((1, member.shape[1]), 1)
    for copy in smalls:
        copy.wait()
    for e in range(examples):
        stratum = strata_s[e]
        live = jnp.where(keep_s[e] == 1, 1, 0)
        owner = table_s[stratum]
        place = taken[owner]
        taken[owner] = place + live
        slot = jnp.where(jnp.logical_and(live == 1, place < CAP), owner * CAP + place, slots)
        chosen[slot] = e
        member[e : e + 1, :] = jnp.where(lane == slots + stratum, live.astype(f32), 0.0)
        dispatch[e : e + 1, :] = jnp.where(jnp.logical_and(lane == slot, lane < slots), 1.0, 0.0)
    rows = []
    for n in range(slots):
        rows.append(pltpu.make_async_copy(hidden.at[chosen[n]], x.at[n], row_sem.at[n]))
        rows.append(
            pltpu.make_async_copy(cotangent.at[chosen[n]], x.at[slots + n], row_sem.at[slots + n])
        )
    for copy in rows + weights[3 + early :]:
        copy.start()

    half = PIECES // 2
    kr = rank_v.shape[0]
    per_row = ROW // wide
    tokens = GROUP * SEQ
    lines = GROUP * half
    spread[...] = (iota((LANES, ROW), 1) // kr == iota((LANES, ROW), 0)).astype(f32).astype(bf16)
    weights[0].wait()
    up_line = iota((per_row * lines, kr), 0)
    pick_up = (per_row * (up_line % half) + up_line // lines == iota((per_row * lines, kr), 1))
    rank_up_rows = nn(pick_up.astype(f32).astype(bf16), rank_v[...]).astype(bf16)
    pick_down = iota((kr * lines, kr), 0) // lines == iota((kr * lines, kr), 1)
    rank_down_rows = nn(pick_down.astype(f32).astype(bf16), rank_v[...]).astype(bf16)
    up_at, up_token = iota((per_row * lines, tokens), 0), iota((per_row * lines, tokens), 1)
    up_mask = (up_at % lines) // half == up_token // SEQ
    down_at, down_token = iota((kr * lines, half * tokens), 0), iota((kr * lines, half * tokens), 1)
    down_mask = jnp.logical_and(
        (down_at % lines) // half == (down_token % tokens) // SEQ, down_at % half == down_token // tokens
    )
    rank_at = iota((lines, ROW), 1) % kr
    for copy in weights[1:3]:
        copy.wait()
    adapters_t[...] = adapters[...].T
    for copy in rows:
        copy.wait()

    for g in range(slots // GROUP):
        model = x.shape[2]
        def both(lo, size):
            return jnp.concatenate(
                [
                    x[g * GROUP : (g + 1) * GROUP, :, lo : lo + size].reshape(tokens, size),
                    x[slots + g * GROUP : slots + (g + 1) * GROUP, :, lo : lo + size].reshape(tokens, size),
                ],
                axis=0,
            )

        for n in range(parts):
            if g == 0:
                weights[3 + n].wait()
            span = pl.ds(n * depth, depth)
            part = nn(both(n * depth, depth), width_v[span, :])
            projected = part if n == 0 else projected + part
            if n == 0:
                adapted = nn(both(0, model), adapters_t[...])
                down_act = adapted[:tokens, :rank].astype(bf16)
                up_back = adapted[tokens:, rank:].astype(bf16)
                left_up = jnp.where(up_mask, nt(rank_up_rows, down_act), 0.0).astype(bf16)
                left_down = nt(rank_down_rows, jnp.concatenate([up_back] * half, axis=0))
                left_down = jnp.where(down_mask, left_down, 0.0).astype(bf16)
        wide_hidden = projected[:tokens].astype(bf16)
        wide_back = projected[tokens:].astype(bf16)
        stacked = jnp.concatenate(
            [wide_hidden[:, n * LANES : (n + 1) * LANES] for n in range(half)], axis=0
        )
        down_grad = nn(left_down, stacked).astype(bf16)
        up_grad = nn(left_up, wide_back)
        up_rows = jnp.concatenate(
            [up_grad[n * lines : (n + 1) * lines] for n in range(per_row)], axis=1
        )
        repeated = nn(down_grad, spread[...])
        down_rows = repeated[:lines]
        for n in range(1, kr):
            down_rows = jnp.where(rank_at == n, repeated[n * lines : (n + 1) * lines], down_rows)

        per_owner = CAP * half
        for n in range(GROUP // CAP):
            owner = g * (GROUP // CAP) + n
            piece = jnp.concatenate(
                [
                    up_rows[n * per_owner : (n + 1) * per_owner],
                    down_rows[n * per_owner : (n + 1) * per_owner],
                ],
                axis=0,
            ).astype(bf16)
            for at in place_of(owner):
                payload[at] = piece


def norm_kernel(
    slots, direct, present, targets, payload, dispatch, member,
    stacked, inverse, picks, counts, sem,
):
    copies = [
        pltpu.make_async_copy(
            targets.at[0, :, pl.ds(n * ROW, ROW)], stacked.at[n], sem.at[n]
        )
        for n in range(PIECES)
    ]
    for copy in copies:
        copy.start()
    total = jnp.zeros((targets.shape[1], LANES), f32)
    for n in range(PIECES):
        copies[n].wait()
        for m in range(ROW // LANES):
            part = stacked[n, :, m * LANES : (m + 1) * LANES].astype(f32)
            total += part * part
    scale = math.sqrt(FEAT) / (TGT // TASKS)
    inverse[...] = jnp.broadcast_to(
        scale * lax.rsqrt(jnp.sum(total, axis=1, keepdims=True) + epsilon), inverse.shape
    )
    owners, pieces = slots // CAP, payload.shape[1]
    step = payload.shape[0] // owners
    values = jnp.concatenate([payload[n * step] for n in range(owners)], axis=0).astype(f32)
    squares = jnp.sum(values * values, axis=1, keepdims=True)
    at = (owners * pieces, picks.shape[1])
    line = iota(at, 0)
    owner = line // pieces
    if direct:
        owner = jnp.bitwise_xor(owner, lax.axis_index("dp"))
    slot = owner * CAP + line % pieces % (pieces // 2) // (PIECES // 2)
    squares = jnp.sum(jnp.where(slot == iota(at, 1), squares, 0.0), axis=0, keepdims=True)
    used = iota(picks.shape, 0) < present[0]
    picks[...] = jnp.where(used, dispatch[...] * lax.rsqrt(squares + epsilon), 0.0)
    held = jnp.sum(jnp.where(used, member[...], 0.0), axis=0, keepdims=True)
    counts[...] = jnp.broadcast_to(held, counts.shape)


def direct_groups(payload, other, *arrived):
    d, x, core = (lax.axis_index(name) for name in ("dp", "x", "core"))
    columns = lax.axis_size("x")

    def place(k, across, on):
        return (jnp.bitwise_xor(d, k) * columns + jnp.bitwise_xor(x, across)) * CORES + on

    pieces = CAP * PIECES
    groups = [(payload[0], place(0, 0, core)), (other[0], place(0, 0, 1 - core))]
    arrived, from_core = arrived[:-1], arrived[-1]
    for on, mine in ((core, True), (1 - core, False)):
        start = 0
        for k, ref in zip(direct_order(lax.axis_size("dp")), arrived):
            span = ref.shape[0]
            rows = ref[...] if mine else from_core[start : start + span]
            start += span
            if k == 0:
                groups.append((rows, place(0, 1, on)))
            else:
                groups.append((rows[:pieces], place(k, on, on)))
                groups.append((rows[pieces:], place(k, on, 1 - on)))
    return groups


def gathered_groups(mine, other):
    core = lax.axis_index("core")
    sources = mine.shape[0]
    groups = []
    step = LANES // (CAP * PIECES)
    for b in range(0, sources, step):
        groups += [(mine[n], n * CORES + core) for n in range(b, b + step)]
        groups += [(other[n], n * CORES + 1 - core) for n in range(b, b + step)]
    return groups


def score_kernel(groups_of, stacked, inverse, counts, *refs):
    back = refs[-1]
    per_task = TGT // TASKS
    half = PIECES // 2
    first = lax.axis_index("dp") * CAP
    share = stacked.shape[1]
    line = iota((1, CORES * LANES), 1)
    piece_of = (line // (CAP * half)) % 2 * half + line % half
    inv = inverse[...]
    pieces = CAP * PIECES
    per_block = CORES * LANES // pieces
    source = iota((per_block, LANES), 0)
    lane = iota((per_block, LANES), 1)
    groups = groups_of(*refs[:-1])
    for b in range(0, len(groups), per_block):
        block = jnp.concatenate([rows for rows, _ in groups[b : b + per_block]], axis=0)
        whole = nt(stacked[...].reshape(PIECES * share, ROW), block)
        products = whole[:share]
        for n in range(1, PIECES):
            products = jnp.where(piece_of == n, whole[n * share : (n + 1) * share], products)
        best = []
        for c in range(CORES):
            total = products[:, c * LANES : (c + 1) * LANES]
            for shift in (1, 2, CAP * half):
                total = total + pltpu.roll(total, LANES - shift, 1)
            total = jnp.maximum(total, 0.0) * inv
            top = jnp.sum(total[:per_task], axis=0, keepdims=True)
            for n in range(1, share // per_task):
                top = jnp.maximum(
                    top, jnp.sum(total[n * per_task : (n + 1) * per_task], axis=0, keepdims=True)
                )
            best.append(top)
        table = jnp.where(source < per_block // CORES, best[0], best[1])
        scores = jnp.broadcast_to(counts[0:1, :], (per_block, counts.shape[1]))
        for n in range(CAP):
            at = lane == source % (per_block // CORES) * pieces + n * half
            column = jnp.sum(jnp.where(at, table, 0.0), axis=1, keepdims=True)
            scores = jnp.where(iota(scores.shape, 1) == first + n, column, scores)
        for n in range(per_block):
            back[groups[b + n][1]] = scores[n : n + 1]


def finish_kernel(slots, strata_total, returned, picks, member, out):
    values = returned[:, 0, :]
    raw = jnp.max(values, axis=0, keepdims=True)
    counts = jnp.sum(values, axis=0, keepdims=True)
    held = iota(counts.shape, 1)
    held = jnp.logical_and(held >= slots, held < slots + strata_total)
    live = jnp.sum(jnp.where(held, counts, 0.0), axis=1, keepdims=True)
    weight = lax.rsqrt(strata_total * jnp.maximum(counts, 1.0))
    picked = jnp.sum(picks[...] * raw, axis=1, keepdims=True)
    picked = picked * jnp.sum(member[...] * weight, axis=1, keepdims=True) * jnp.sqrt(live)
    examples = picks.shape[0]
    square = iota((examples, LANES), 0) == iota((examples, LANES), 1)
    out[...] = jnp.sum(jnp.where(square, picked, 0.0), axis=0)[:examples]


def direct_order(owners):
    return [2, 1, 0, 3] if owners == 4 else [1, 0]


def direct_rows(payload, owners, columns, norms):
    swap = [(n, n ^ 1) for n in range(CORES)]
    other = lax.ppermute(payload, "core", swap)
    arrived = []
    for k in direct_order(owners):
        pairs = []
        for d in range(owners):
            for x in range(columns):
                for c in range(CORES):
                    to = (d ^ k, x ^ (1 if k == 0 else c), c)
                    pairs.append(
                        ((d * columns + x) * CORES + c, (to[0] * columns + to[1]) * CORES + to[2])
                    )
        rows = payload[0] if k == 0 else jnp.concatenate([payload[k], other[k]], axis=0)
        arrived.append(lax.ppermute(rows, ("dp", "x", "core"), pairs))
    arrived, norms = lax.optimization_barrier((arrived, norms))
    from_core = lax.ppermute(jnp.concatenate(arrived, axis=0), "core", swap)
    return [payload, other] + arrived + [from_core], norms


def shards(
    hidden,
    cotangent,
    adapter_down_weight,
    adapter_up_weight,
    width_projection_factor,
    rank_projection_factor,
    targets,
    strata,
    keep,
    shard_example_count,
    stratum_owner_table,
):
    examples = strata.shape[0]
    strata_total = stratum_owner_table.shape[0]
    owners, columns = lax.axis_size("dp"), lax.axis_size("x")
    slots = owners * CAP
    model, wide = width_projection_factor.shape
    rank, kr = rank_projection_factor.shape
    share = targets.shape[1]
    chips = owners * columns
    direct = columns == 2 and owners in (2, 4)

    def places(owner):
        if direct:
            return [jnp.bitwise_xor(lax.axis_index("dp"), owner)]
        return [owner * columns + n for n in range(columns)]

    lanes = -(-(slots + strata_total) // LANES) * LANES

    payload, dispatch, member = pl.pallas_call(
        functools.partial(project_kernel, places),
        out_shape=(
            jax.ShapeDtypeStruct((owners if direct else chips, CAP * PIECES, ROW), bf16),
            jax.ShapeDtypeStruct((examples, lanes), f32),
            jax.ShapeDtypeStruct((examples, lanes), f32),
        ),
        in_specs=[HBM] * 9,
        out_specs=(VMEM,) * 3,
        scratch_shapes=[
            pltpu.SMEM((examples,), i32),
            pltpu.SMEM((examples,), i32),
            pltpu.SMEM((strata_total,), i32),
            pltpu.SMEM((owners,), i32),
            pltpu.SMEM((slots + 1,), i32),
            pltpu.VMEM((2 * slots, SEQ, model), bf16),
            pltpu.VMEM((2 * rank, model), bf16),
            pltpu.VMEM((model, 2 * rank), bf16),
            pltpu.VMEM((model, wide), bf16),
            pltpu.VMEM((kr, rank), bf16),
            pltpu.VMEM((LANES, ROW), bf16),
            pltpu.SemaphoreType.DMA((3,)),
            pltpu.SemaphoreType.DMA((2 * slots,)),
            pltpu.SemaphoreType.DMA((7,)),
        ],
        compiler_params=pltpu.CompilerParams(vmem_limit_bytes=40 * 2**20),
        name="project",
    )(
        *in_hbm(
            strata,
            keep,
            stratum_owner_table,
            hidden.reshape(examples, SEQ, model),
            cotangent.reshape(examples, SEQ, model),
            adapter_down_weight.T,
            adapter_up_weight,
            width_projection_factor,
            rank_projection_factor.T,
        )
    )
    stacked, inverse, picks, counts = pl.pallas_call(
        functools.partial(norm_kernel, slots, direct),
        out_shape=(
            jax.ShapeDtypeStruct((PIECES, share, ROW), bf16),
            jax.ShapeDtypeStruct((share, LANES), f32),
            jax.ShapeDtypeStruct((examples, lanes), f32),
            jax.ShapeDtypeStruct((8, lanes), f32),
        ),
        in_specs=[
            pl.BlockSpec(memory_space=pltpu.SMEM), HBM, VMEM, VMEM, VMEM
        ],
        out_specs=(VMEM,) * 4,
        scratch_shapes=[pltpu.SemaphoreType.DMA((PIECES,))],
        compiler_params=pltpu.CompilerParams(vmem_limit_bytes=20 * 2**20),
        cost_estimate=pl.CostEstimate(flops=4 * share * FEAT, bytes_accessed=4 * share * FEAT, transcendentals=0),
        name="norms",
    )(shard_example_count, *in_hbm(targets), payload, dispatch, member)
    if direct:
        rows, (stacked, inverse, picks, counts) = direct_rows(payload, owners, columns, (stacked, inverse, picks, counts))
    else:
        mine = lax.all_to_all(payload, ("dp", "x"), split_axis=0, concat_axis=0, tiled=True)
        rows = [mine, lax.ppermute(mine, "core", [(n, n ^ 1) for n in range(CORES)])]
    back = pl.pallas_call(
        functools.partial(score_kernel, direct_groups if direct else gathered_groups),
        out_shape=jax.ShapeDtypeStruct((chips * CORES, 1, lanes), f32),
        in_specs=[VMEM] * (3 + len(rows)),
        out_specs=VMEM,
        compiler_params=pltpu.CompilerParams(vmem_limit_bytes=40 * 2**20),
        name="score",
    )(stacked, inverse, counts, *rows)
    returned = lax.all_to_all(back, ("dp", "x", "core"), split_axis=0, concat_axis=0, tiled=True)
    return pl.pallas_call(
        functools.partial(finish_kernel, slots, strata_total),
        out_shape=jax.ShapeDtypeStruct((examples,), f32),
        in_specs=[VMEM] * 3,
        out_specs=VMEM,
        compiler_params=pltpu.CompilerParams(vmem_limit_bytes=4 * 2**20),
        name="finish",
    )(returned, picks, member)


def solution(mesh):
    sizes = [mesh.shape[name] for name in ("groups", "dp", "tgt")]
    fine = jax.sharding.Mesh(
        mesh.devices.reshape(sizes[0], sizes[1], sizes[2] // CORES, CORES),
        ("groups", "dp", "x", "core"),
    )
    every = P(("groups", "dp", "x", "core"))
    whole = P()
    return jax.shard_map(
        shards,
        mesh=fine,
        in_specs=(
            every, every, whole, whole, whole, whole,
            P(("groups", "dp"), ("x", "core"), None),
            every, every, every, whole,
        ),
        out_specs=every,
        check_vma=False,
    )
```

```python
import functools
import math

import jax
import jax.numpy as jnp
from jax import lax
from jax.experimental import pallas as pl
from jax.experimental.pallas import tpu as pltpu
from jax.sharding import PartitionSpec as P

FEAT = 8192
CAP = 2
TGT = 768
TASKS = 16
SEQ = 8
CORES = 2
SWAP = [(0, 1), (1, 0)]
LANES = 128
ROW = 1024
PIECES = FEAT // ROW
GROUP = 8
epsilon = 1e-06
bf16, f32, i32 = jnp.bfloat16, jnp.float32, jnp.int32

HBM = pl.BlockSpec(memory_space=pltpu.HBM)
VMEM = pl.BlockSpec(memory_space=pltpu.VMEM)


def nn(a, b):
    return jnp.dot(a, b, preferred_element_type=f32)


def nt(a, b):
    return lax.dot_general(a, b, (((1,), (1,)), ((), ())), preferred_element_type=f32)


def in_hbm(*arrays):
    return [pltpu.with_memory_space_constraint(a, pltpu.HBM) for a in arrays]


def iota(shape, dim):
    return lax.broadcasted_iota(i32, shape, dim)


def project_kernel(
    place_of, strata, keep, table, hidden, cotangent, down_t, up, width, rank_t,
    payload, dispatch, member,
    strata_s, keep_s, table_s, taken, chosen, x, adapters, adapters_t, width_v, rank_v, spread,
    small_sem, row_sem, weight_sem,
):
    examples, strata_total = strata_s.shape[0], table_s.shape[0]
    slots = x.shape[0] // 2
    owners = slots // CAP
    rank = down_t.shape[0]
    wide = width.shape[1]
    parts = 2
    early = 1
    depth = width.shape[0] // parts

    smalls = [
        pltpu.make_async_copy(a, b, small_sem.at[n])
        for n, (a, b) in enumerate(
            [(strata, strata_s), (keep, keep_s), (table, table_s)]
        )
    ]
    weights = [
        pltpu.make_async_copy(rank_t, rank_v, weight_sem.at[0]),
        pltpu.make_async_copy(down_t, adapters.at[pl.ds(0, rank)], weight_sem.at[1]),
        pltpu.make_async_copy(up, adapters.at[pl.ds(rank, rank)], weight_sem.at[2]),
    ] + [
        pltpu.make_async_copy(
            width.at[pl.ds(n * depth, depth)], width_v.at[pl.ds(n * depth, depth)], weight_sem.at[3 + n]
        )
        for n in range(parts)
    ]
    for copy in smalls + weights[: 3 + early]:
        copy.start()

    for n in range(owners):
        taken[n] = 0
    for n in range(slots + 1):
        chosen[n] = 0
    lane = iota((1, member.shape[1]), 1)
    for copy in smalls:
        copy.wait()
    for e in range(examples):
        stratum = strata_s[e]
        live = jnp.where(keep_s[e] == 1, 1, 0)
        owner = table_s[stratum]
        place = taken[owner]
        taken[owner] = place + live
        slot = jnp.where(jnp.logical_and(live == 1, place < CAP), owner * CAP + place, slots)
        chosen[slot] = e
        member[e : e + 1, :] = jnp.where(lane == slots + stratum, live.astype(f32), 0.0)
        dispatch[e : e + 1, :] = jnp.where(jnp.logical_and(lane == slot, lane < slots), 1.0, 0.0)
    rows = []
    for n in range(slots):
        rows.append(pltpu.make_async_copy(hidden.at[chosen[n]], x.at[n], row_sem.at[n]))
        rows.append(
            pltpu.make_async_copy(cotangent.at[chosen[n]], x.at[slots + n], row_sem.at[slots + n])
        )
    for copy in rows + weights[3 + early :]:
        copy.start()

    half = PIECES // 2
    kr = rank_v.shape[0]
    per_row = ROW // wide
    tokens = GROUP * SEQ
    lines = GROUP * half
    spread[...] = (iota((LANES, ROW), 1) // kr == iota((LANES, ROW), 0)).astype(f32).astype(bf16)
    weights[0].wait()
    up_line = iota((per_row * lines, kr), 0)
    pick_up = (per_row * (up_line % half) + up_line // lines == iota((per_row * lines, kr), 1))
    rank_up_rows = nn(pick_up.astype(f32).astype(bf16), rank_v[...]).astype(bf16)
    pick_down = iota((kr * lines, kr), 0) // lines == iota((kr * lines, kr), 1)
    rank_down_rows = nn(pick_down.astype(f32).astype(bf16), rank_v[...]).astype(bf16)
    up_at, up_token = iota((per_row * lines, tokens), 0), iota((per_row * lines, tokens), 1)
    up_mask = (up_at % lines) // half == up_token // SEQ
    down_at, down_token = iota((kr * lines, half * tokens), 0), iota((kr * lines, half * tokens), 1)
    down_mask = jnp.logical_and(
        (down_at % lines) // half == (down_token % tokens) // SEQ, down_at % half == down_token // tokens
    )
    rank_at = iota((lines, ROW), 1) % kr
    for copy in weights[1:3]:
        copy.wait()
    adapters_t[...] = adapters[...].T
    for copy in rows:
        copy.wait()

    for g in range(slots // GROUP):
        model = x.shape[2]
        def both(lo, size):
            return jnp.concatenate(
                [
                    x[g * GROUP : (g + 1) * GROUP, :, lo : lo + size].reshape(tokens, size),
                    x[slots + g * GROUP : slots + (g + 1) * GROUP, :, lo : lo + size].reshape(tokens, size),
                ],
                axis=0,
            )

        for n in range(parts):
            if g == 0:
                weights[3 + n].wait()
            span = pl.ds(n * depth, depth)
            part = nn(both(n * depth, depth), width_v[span, :])
            projected = part if n == 0 else projected + part
            if n == 0:
                adapted = nn(both(0, model), adapters_t[...])
                down_act = adapted[:tokens, :rank].astype(bf16)
                up_back = adapted[tokens:, rank:].astype(bf16)
                left_up = jnp.where(up_mask, nt(rank_up_rows, down_act), 0.0).astype(bf16)
                left_down = nt(rank_down_rows, jnp.concatenate([up_back] * half, axis=0))
                left_down = jnp.where(down_mask, left_down, 0.0).astype(bf16)
        wide_hidden = projected[:tokens].astype(bf16)
        wide_back = projected[tokens:].astype(bf16)
        stacked = jnp.concatenate(
            [wide_hidden[:, n * LANES : (n + 1) * LANES] for n in range(half)], axis=0
        )
        down_grad = nn(left_down, stacked).astype(bf16)
        up_grad = nn(left_up, wide_back)
        up_rows = jnp.concatenate(
            [up_grad[n * lines : (n + 1) * lines] for n in range(per_row)], axis=1
        )
        repeated = nn(down_grad, spread[...])
        down_rows = repeated[:lines]
        for n in range(1, kr):
            down_rows = jnp.where(rank_at == n, repeated[n * lines : (n + 1) * lines], down_rows)

        per_owner = CAP * half
        for n in range(GROUP // CAP):
            owner = g * (GROUP // CAP) + n
            piece = jnp.concatenate(
                [
                    up_rows[n * per_owner : (n + 1) * per_owner],
                    down_rows[n * per_owner : (n + 1) * per_owner],
                ],
                axis=0,
            ).astype(bf16)
            for at in place_of(owner):
                payload[at] = piece


def norm_kernel(
    slots, direct, present, targets, payload, dispatch, member,
    stacked, inverse, picks, counts, sem,
):
    copies = [
        pltpu.make_async_copy(
            targets.at[0, :, pl.ds(n * ROW, ROW)], stacked.at[n], sem.at[n]
        )
        for n in range(PIECES)
    ]
    for copy in copies:
        copy.start()
    total = jnp.zeros((targets.shape[1], LANES), f32)
    for n in range(PIECES):
        copies[n].wait()
        for m in range(ROW // LANES):
            part = stacked[n, :, m * LANES : (m + 1) * LANES].astype(f32)
            total += part * part
    scale = math.sqrt(FEAT) / (TGT // TASKS)
    inverse[...] = jnp.broadcast_to(
        scale * lax.rsqrt(jnp.sum(total, axis=1, keepdims=True) + epsilon), inverse.shape
    )
    owners, pieces = slots // CAP, payload.shape[1]
    step = payload.shape[0] // owners
    values = jnp.concatenate([payload[n * step] for n in range(owners)], axis=0).astype(f32)
    squares = jnp.sum(values * values, axis=1, keepdims=True)
    at = (owners * pieces, picks.shape[1])
    line = iota(at, 0)
    owner = line // pieces
    if direct:
        owner = jnp.bitwise_xor(owner, lax.axis_index("dp"))
    slot = owner * CAP + line % pieces % (pieces // 2) // (PIECES // 2)
    squares = jnp.sum(jnp.where(slot == iota(at, 1), squares, 0.0), axis=0, keepdims=True)
    used = iota(picks.shape, 0) < present[0]
    picks[...] = jnp.where(used, dispatch[...] * lax.rsqrt(squares + epsilon), 0.0)
    held = jnp.sum(jnp.where(used, member[...], 0.0), axis=0, keepdims=True)
    counts[...] = jnp.broadcast_to(held, counts.shape)


def direct_groups(payload, other, *arrived):
    d, x, core = (lax.axis_index(name) for name in ("dp", "x", "core"))
    columns = lax.axis_size("x")

    def place(k, across, on):
        return (jnp.bitwise_xor(d, k) * columns + jnp.bitwise_xor(x, across)) * CORES + on

    pieces = CAP * PIECES
    groups = [(payload[0], place(0, 0, core)), (other[0], place(0, 0, 1 - core))]
    arrived, from_core = arrived[:-1], arrived[-1]
    for on, mine in ((core, True), (1 - core, False)):
        start = 0
        for k, ref in zip(direct_order(lax.axis_size("dp")), arrived):
            span = ref.shape[0]
            rows = ref[...] if mine else from_core[start : start + span]
            start += span
            if k == 0:
                groups.append((rows, place(0, 1, on)))
            else:
                groups.append((rows[:pieces], place(k, on, on)))
                groups.append((rows[pieces:], place(k, on, 1 - on)))
    return groups


def gathered_groups(mine, other):
    core = lax.axis_index("core")
    sources = mine.shape[0]
    groups = []
    step = LANES // (CAP * PIECES)
    for b in range(0, sources, step):
        groups += [(mine[n], n * CORES + core) for n in range(b, b + step)]
        groups += [(other[n], n * CORES + 1 - core) for n in range(b, b + step)]
    return groups


def score_kernel(groups_of, stacked, inverse, counts, *refs):
    back = refs[-1]
    per_task = TGT // TASKS
    half = PIECES // 2
    first = lax.axis_index("dp") * CAP
    share = stacked.shape[1]
    line = iota((1, CORES * LANES), 1)
    piece_of = (line // (CAP * half)) % 2 * half + line % half
    inv = inverse[...]
    pieces = CAP * PIECES
    per_block = CORES * LANES // pieces
    source = iota((per_block, LANES), 0)
    lane = iota((per_block, LANES), 1)
    groups = groups_of(*refs[:-1])
    for b in range(0, len(groups), per_block):
        block = jnp.concatenate([rows for rows, _ in groups[b : b + per_block]], axis=0)
        whole = nt(stacked[...].reshape(PIECES * share, ROW), block)
        products = whole[:share]
        for n in range(1, PIECES):
            products = jnp.where(piece_of == n, whole[n * share : (n + 1) * share], products)
        best = []
        for c in range(CORES):
            total = products[:, c * LANES : (c + 1) * LANES]
            for shift in (1, 2, CAP * half):
                total = total + pltpu.roll(total, LANES - shift, 1)
            total = jnp.maximum(total, 0.0) * inv
            top = jnp.sum(total[:per_task], axis=0, keepdims=True)
            for n in range(1, share // per_task):
                top = jnp.maximum(
                    top, jnp.sum(total[n * per_task : (n + 1) * per_task], axis=0, keepdims=True)
                )
            best.append(top)
        table = jnp.where(source < per_block // CORES, best[0], best[1])
        scores = jnp.broadcast_to(counts[0:1, :], (per_block, counts.shape[1]))
        for n in range(CAP):
            at = lane == source % (per_block // CORES) * pieces + n * half
            column = jnp.sum(jnp.where(at, table, 0.0), axis=1, keepdims=True)
            scores = jnp.where(iota(scores.shape, 1) == first + n, column, scores)
        for n in range(per_block):
            back[groups[b + n][1]] = scores[n : n + 1]


def finish_kernel(slots, strata_total, direct, picks, member, *refs):
    returned, out = refs[:-1], refs[-1]
    if direct:
        d, x, core = (lax.axis_index(name) for name in ("dp", "x", "core"))
        place = (d * lax.axis_size("x") + x) * CORES + core
        values = jnp.concatenate([ref[place] for ref in returned], axis=0)
    else:
        values = returned[0][:, 0, :]
    raw = jnp.max(values, axis=0, keepdims=True)
    counts = jnp.sum(values, axis=0, keepdims=True)
    held = iota(counts.shape, 1)
    held = jnp.logical_and(held >= slots, held < slots + strata_total)
    live = jnp.sum(jnp.where(held, counts, 0.0), axis=1, keepdims=True)
    weight = lax.rsqrt(strata_total * jnp.maximum(counts, 1.0))
    picked = jnp.sum(picks[...] * raw, axis=1, keepdims=True)
    picked = picked * jnp.sum(member[...] * weight, axis=1, keepdims=True) * jnp.sqrt(live)
    examples = picks.shape[0]
    square = iota((examples, LANES), 0) == iota((examples, LANES), 1)
    out[...] = jnp.sum(jnp.where(square, picked, 0.0), axis=0)[:examples]


def direct_order(owners):
    return [2, 1, 0, 3] if owners == 4 else [1, 0]


def direct_pairs(k, owners, columns):
    pairs = []
    for d in range(owners):
        for x in range(columns):
            for c in range(CORES):
                to = (d ^ k, x ^ (1 if k == 0 else c), c)
                pairs.append(
                    ((d * columns + x) * CORES + c, (to[0] * columns + to[1]) * CORES + to[2])
                )
    return pairs


def direct_return(back, owners, columns, slots):
    def merge(a, b):
        return jnp.where(iota(a.shape, 2) < slots, jnp.maximum(a, b), a + b)

    chip = merge(back, lax.ppermute(back, "core", SWAP))
    order = [3, 1, 2, 0] if owners == 4 else [1, 0]
    got = [lax.ppermute(chip, ("dp", "x", "core"), direct_pairs(k, owners, columns)) for k in order]
    far = functools.reduce(merge, [part for k, part in zip(order, got) if k > 0])
    return [chip, got[order.index(0)], far, lax.ppermute(far, "core", SWAP)]


def direct_rows(payload, owners, columns, norms):
    other = lax.ppermute(payload, "core", SWAP)
    arrived = []
    for k in direct_order(owners):
        rows = payload[0] if k == 0 else jnp.concatenate([payload[k], other[k]], axis=0)
        arrived.append(lax.ppermute(rows, ("dp", "x", "core"), direct_pairs(k, owners, columns)))
    arrived, norms = lax.optimization_barrier((arrived, norms))
    from_core = lax.ppermute(jnp.concatenate(arrived, axis=0), "core", SWAP)
    return [payload, other] + arrived + [from_core], norms


def shards(
    hidden,
    cotangent,
    adapter_down_weight,
    adapter_up_weight,
    width_projection_factor,
    rank_projection_factor,
    targets,
    strata,
    keep,
    shard_example_count,
    stratum_owner_table,
):
    examples = strata.shape[0]
    strata_total = stratum_owner_table.shape[0]
    owners, columns = lax.axis_size("dp"), lax.axis_size("x")
    slots = owners * CAP
    model, wide = width_projection_factor.shape
    rank, kr = rank_projection_factor.shape
    share = targets.shape[1]
    chips = owners * columns
    direct = columns == 2 and owners in (2, 4)

    def places(owner):
        if direct:
            return [jnp.bitwise_xor(lax.axis_index("dp"), owner)]
        return [owner * columns + n for n in range(columns)]

    lanes = -(-(slots + strata_total) // LANES) * LANES

    payload, dispatch, member = pl.pallas_call(
        functools.partial(project_kernel, places),
        out_shape=(
            jax.ShapeDtypeStruct((owners if direct else chips, CAP * PIECES, ROW), bf16),
            jax.ShapeDtypeStruct((examples, lanes), f32),
            jax.ShapeDtypeStruct((examples, lanes), f32),
        ),
        in_specs=[HBM] * 9,
        out_specs=(VMEM,) * 3,
        scratch_shapes=[
            pltpu.SMEM((examples,), i32),
            pltpu.SMEM((examples,), i32),
            pltpu.SMEM((strata_total,), i32),
            pltpu.SMEM((owners,), i32),
            pltpu.SMEM((slots + 1,), i32),
            pltpu.VMEM((2 * slots, SEQ, model), bf16),
            pltpu.VMEM((2 * rank, model), bf16),
            pltpu.VMEM((model, 2 * rank), bf16),
            pltpu.VMEM((model, wide), bf16),
            pltpu.VMEM((kr, rank), bf16),
            pltpu.VMEM((LANES, ROW), bf16),
            pltpu.SemaphoreType.DMA((3,)),
            pltpu.SemaphoreType.DMA((2 * slots,)),
            pltpu.SemaphoreType.DMA((7,)),
        ],
        compiler_params=pltpu.CompilerParams(vmem_limit_bytes=40 * 2**20),
        name="project",
    )(
        *in_hbm(
            strata,
            keep,
            stratum_owner_table,
            hidden.reshape(examples, SEQ, model),
            cotangent.reshape(examples, SEQ, model),
            adapter_down_weight.T,
            adapter_up_weight,
            width_projection_factor,
            rank_projection_factor.T,
        )
    )
    stacked, inverse, picks, counts = pl.pallas_call(
        functools.partial(norm_kernel, slots, direct),
        out_shape=(
            jax.ShapeDtypeStruct((PIECES, share, ROW), bf16),
            jax.ShapeDtypeStruct((share, LANES), f32),
            jax.ShapeDtypeStruct((examples, lanes), f32),
            jax.ShapeDtypeStruct((8, lanes), f32),
        ),
        in_specs=[
            pl.BlockSpec(memory_space=pltpu.SMEM), HBM, VMEM, VMEM, VMEM
        ],
        out_specs=(VMEM,) * 4,
        scratch_shapes=[pltpu.SemaphoreType.DMA((PIECES,))],
        compiler_params=pltpu.CompilerParams(vmem_limit_bytes=20 * 2**20),
        cost_estimate=pl.CostEstimate(flops=4 * share * FEAT, bytes_accessed=4 * share * FEAT, transcendentals=0),
        name="norms",
    )(shard_example_count, *in_hbm(targets), payload, dispatch, member)
    if direct:
        rows, (stacked, inverse, picks, counts) = direct_rows(payload, owners, columns, (stacked, inverse, picks, counts))
    else:
        mine = lax.all_to_all(payload, ("dp", "x"), split_axis=0, concat_axis=0, tiled=True)
        rows = [mine, lax.ppermute(mine, "core", SWAP)]
    back = pl.pallas_call(
        functools.partial(score_kernel, direct_groups if direct else gathered_groups),
        out_shape=jax.ShapeDtypeStruct((chips * CORES, 1, lanes), f32),
        in_specs=[VMEM] * (3 + len(rows)),
        out_specs=VMEM,
        compiler_params=pltpu.CompilerParams(vmem_limit_bytes=40 * 2**20),
        name="score",
    )(stacked, inverse, counts, *rows)
    if direct:
        returned = direct_return(back, owners, columns, slots)
    else:
        returned = [
            lax.all_to_all(back, ("dp", "x", "core"), split_axis=0, concat_axis=0, tiled=True)
        ]
    return pl.pallas_call(
        functools.partial(finish_kernel, slots, strata_total, direct),
        out_shape=jax.ShapeDtypeStruct((examples,), f32),
        in_specs=[VMEM] * (2 + len(returned)),
        out_specs=VMEM,
        compiler_params=pltpu.CompilerParams(vmem_limit_bytes=4 * 2**20),
        name="finish",
    )(picks, member, *returned)


def solution(mesh):
    sizes = [mesh.shape[name] for name in ("groups", "dp", "tgt")]
    fine = jax.sharding.Mesh(
        mesh.devices.reshape(sizes[0], sizes[1], sizes[2] // CORES, CORES),
        ("groups", "dp", "x", "core"),
    )
    every = P(("groups", "dp", "x", "core"))
    whole = P()
    return jax.shard_map(
        shards,
        mesh=fine,
        in_specs=(
            every, every, whole, whole, whole, whole,
            P(("groups", "dp"), ("x", "core"), None),
            every, every, every, whole,
        ),
        out_specs=every,
        check_vma=False,
    )
```

```python
import functools
import math

import jax
import jax.numpy as jnp
from jax import lax
from jax.experimental import pallas as pl
from jax.experimental.pallas import tpu as pltpu
from jax.sharding import PartitionSpec as P

FEAT = 8192
CAP = 2
TGT = 768
TASKS = 16
SEQ = 8
CORES = 2
SWAP = [(0, 1), (1, 0)]
LANES = 128
ROW = 1024
PIECES = FEAT // ROW
GROUP = 8
epsilon = 1e-06
bf16, f32, i32 = jnp.bfloat16, jnp.float32, jnp.int32

HBM = pl.BlockSpec(memory_space=pltpu.HBM)
VMEM = pl.BlockSpec(memory_space=pltpu.VMEM)


def nn(a, b):
    return jnp.dot(a, b, preferred_element_type=f32)


def nt(a, b):
    return lax.dot_general(a, b, (((1,), (1,)), ((), ())), preferred_element_type=f32)


def in_hbm(*arrays):
    return [pltpu.with_memory_space_constraint(a, pltpu.HBM) for a in arrays]


def iota(shape, dim):
    return lax.broadcasted_iota(i32, shape, dim)


def project_kernel(
    place_of, strata, keep, table, hidden, cotangent, down_t, up, width, rank_t,
    payload, dispatch, member,
    strata_s, keep_s, table_s, taken, chosen, x, adapters, adapters_t, width_v, rank_v, spread,
    small_sem, row_sem, weight_sem,
):
    examples, strata_total = strata_s.shape[0], table_s.shape[0]
    slots = x.shape[0] // 2
    owners = slots // CAP
    rank = down_t.shape[0]
    wide = width.shape[1]
    parts = 2
    early = 1
    depth = width.shape[0] // parts

    smalls = [
        pltpu.make_async_copy(a, b, small_sem.at[n])
        for n, (a, b) in enumerate(
            [(strata, strata_s), (keep, keep_s), (table, table_s)]
        )
    ]
    weights = [
        pltpu.make_async_copy(rank_t, rank_v, weight_sem.at[0]),
        pltpu.make_async_copy(down_t, adapters.at[pl.ds(0, rank)], weight_sem.at[1]),
        pltpu.make_async_copy(up, adapters.at[pl.ds(rank, rank)], weight_sem.at[2]),
    ] + [
        pltpu.make_async_copy(
            width.at[pl.ds(n * depth, depth)], width_v.at[pl.ds(n * depth, depth)], weight_sem.at[3 + n]
        )
        for n in range(parts)
    ]
    for copy in smalls + weights[: 3 + early]:
        copy.start()

    for n in range(owners):
        taken[n] = 0
    for n in range(slots + 1):
        chosen[n] = 0
    lane = iota((1, member.shape[1]), 1)
    for copy in smalls:
        copy.wait()
    for e in range(examples):
        stratum = strata_s[e]
        live = jnp.where(keep_s[e] == 1, 1, 0)
        owner = table_s[stratum]
        place = taken[owner]
        taken[owner] = place + live
        slot = jnp.where(jnp.logical_and(live == 1, place < CAP), owner * CAP + place, slots)
        chosen[slot] = e
        member[e : e + 1, :] = jnp.where(lane == slots + stratum, live.astype(f32), 0.0)
        dispatch[e : e + 1, :] = jnp.where(jnp.logical_and(lane == slot, lane < slots), 1.0, 0.0)
    rows = []
    for n in range(slots):
        rows.append(pltpu.make_async_copy(hidden.at[chosen[n]], x.at[n], row_sem.at[n]))
        rows.append(
            pltpu.make_async_copy(cotangent.at[chosen[n]], x.at[slots + n], row_sem.at[slots + n])
        )
    for copy in rows + weights[3 + early :]:
        copy.start()

    half = PIECES // 2
    kr = rank_v.shape[0]
    per_row = ROW // wide
    tokens = GROUP * SEQ
    lines = GROUP * half
    spread[...] = (iota((LANES, ROW), 1) // kr == iota((LANES, ROW), 0)).astype(f32).astype(bf16)
    weights[0].wait()
    up_line = iota((per_row * lines, kr), 0)
    pick_up = (per_row * (up_line % half) + up_line // lines == iota((per_row * lines, kr), 1))
    rank_up_rows = nn(pick_up.astype(f32).astype(bf16), rank_v[...]).astype(bf16)
    pick_down = iota((kr * lines, kr), 0) // lines == iota((kr * lines, kr), 1)
    rank_down_rows = nn(pick_down.astype(f32).astype(bf16), rank_v[...]).astype(bf16)
    up_at, up_token = iota((per_row * lines, tokens), 0), iota((per_row * lines, tokens), 1)
    up_mask = (up_at % lines) // half == up_token // SEQ
    down_at, down_token = iota((kr * lines, half * tokens), 0), iota((kr * lines, half * tokens), 1)
    down_mask = jnp.logical_and(
        (down_at % lines) // half == (down_token % tokens) // SEQ, down_at % half == down_token // tokens
    )
    rank_at = iota((lines, ROW), 1) % kr
    for copy in weights[1:3]:
        copy.wait()
    adapters_t[...] = adapters[...].T
    for copy in rows:
        copy.wait()

    for g in range(slots // GROUP):
        model = x.shape[2]
        def both(lo, size):
            return jnp.concatenate(
                [
                    x[g * GROUP : (g + 1) * GROUP, :, lo : lo + size].reshape(tokens, size),
                    x[slots + g * GROUP : slots + (g + 1) * GROUP, :, lo : lo + size].reshape(tokens, size),
                ],
                axis=0,
            )

        for n in range(parts):
            if g == 0:
                weights[3 + n].wait()
            span = pl.ds(n * depth, depth)
            part = nn(both(n * depth, depth), width_v[span, :])
            projected = part if n == 0 else projected + part
            if n == 0:
                adapted = nn(both(0, model), adapters_t[...])
                down_act = adapted[:tokens, :rank].astype(bf16)
                up_back = adapted[tokens:, rank:].astype(bf16)
                left_up = jnp.where(up_mask, nt(rank_up_rows, down_act), 0.0).astype(bf16)
                left_down = nt(rank_down_rows, jnp.concatenate([up_back] * half, axis=0))
                left_down = jnp.where(down_mask, left_down, 0.0).astype(bf16)
        wide_hidden = projected[:tokens].astype(bf16)
        wide_back = projected[tokens:].astype(bf16)
        stacked = jnp.concatenate(
            [wide_hidden[:, n * LANES : (n + 1) * LANES] for n in range(half)], axis=0
        )
        down_grad = nn(left_down, stacked).astype(bf16)
        up_grad = nn(left_up, wide_back)
        up_rows = jnp.concatenate(
            [up_grad[n * lines : (n + 1) * lines] for n in range(per_row)], axis=1
        )
        repeated = nn(down_grad, spread[...])
        down_rows = repeated[:lines]
        for n in range(1, kr):
            down_rows = jnp.where(rank_at == n, repeated[n * lines : (n + 1) * lines], down_rows)

        per_owner = CAP * half
        for n in range(GROUP // CAP):
            owner = g * (GROUP // CAP) + n
            piece = jnp.concatenate(
                [
                    up_rows[n * per_owner : (n + 1) * per_owner],
                    down_rows[n * per_owner : (n + 1) * per_owner],
                ],
                axis=0,
            ).astype(bf16)
            for at in place_of(owner):
                payload[at] = piece


def norm_kernel(
    slots, direct, present, targets, payload, dispatch, member,
    stacked, inverse, picks, counts, sem,
):
    copies = [
        pltpu.make_async_copy(
            targets.at[0, :, pl.ds(n * ROW, ROW)], stacked.at[n], sem.at[n]
        )
        for n in range(PIECES)
    ]
    for copy in copies:
        copy.start()
    total = jnp.zeros((targets.shape[1], LANES), f32)
    for n in range(PIECES):
        copies[n].wait()
        for m in range(ROW // LANES):
            part = stacked[n, :, m * LANES : (m + 1) * LANES].astype(f32)
            total += part * part
    scale = math.sqrt(FEAT) / (TGT // TASKS)
    inverse[...] = jnp.broadcast_to(
        scale * lax.rsqrt(jnp.sum(total, axis=1, keepdims=True) + epsilon), inverse.shape
    )
    owners, pieces = slots // CAP, payload.shape[1]
    step = payload.shape[0] // owners
    values = jnp.concatenate([payload[n * step] for n in range(owners)], axis=0).astype(f32)
    squares = jnp.sum(values * values, axis=1, keepdims=True)
    at = (owners * pieces, picks.shape[1])
    line = iota(at, 0)
    owner = line // pieces
    if direct:
        owner = jnp.bitwise_xor(owner, lax.axis_index("dp"))
    slot = owner * CAP + line % pieces % (pieces // 2) // (PIECES // 2)
    squares = jnp.sum(jnp.where(slot == iota(at, 1), squares, 0.0), axis=0, keepdims=True)
    used = iota(picks.shape, 0) < present[0]
    picks[...] = jnp.where(used, dispatch[...] * lax.rsqrt(squares + epsilon), 0.0)
    held = jnp.sum(jnp.where(used, member[...], 0.0), axis=0, keepdims=True)
    counts[...] = jnp.broadcast_to(held, counts.shape)


def direct_groups(payload, other, *arrived):
    core = lax.axis_index("core")
    pieces = CAP * PIECES
    home = lambda n, on: [(0, (n, on)), (1, (n, on))]
    groups = [(payload[0], home(0, core)), (other[0], home(0, 1 - core))]
    arrived, from_core = arrived[:-1], arrived[-1]
    for out, on in ((0, core), (1, 1 - core)):
        start = 0
        for k, ref in zip(direct_order(lax.axis_size("dp")), arrived):
            span = ref.shape[0]
            rows = from_core[start : start + span] if out else ref[...]
            start += span
            if k == 0:
                groups.append((rows, home(1, on)))
            else:
                groups.append((rows[:pieces], [(out, (1 + k, on))]))
                groups.append((rows[pieces:], [(out, (1 + k, 1 - on))]))
    return groups


def gathered_groups(mine, other):
    core = lax.axis_index("core")
    sources = mine.shape[0]
    groups = []
    step = LANES // (CAP * PIECES)
    for b in range(0, sources, step):
        groups += [(mine[n], [(0, (n * CORES + core,))]) for n in range(b, b + step)]
        groups += [(other[n], [(0, (n * CORES + 1 - core,))]) for n in range(b, b + step)]
    return groups


def score_kernel(groups_of, outs, stacked, inverse, counts, *refs):
    rows, back = refs[:-outs], refs[-outs:]
    per_task = TGT // TASKS
    half = PIECES // 2
    first = lax.axis_index("dp") * CAP
    share = stacked.shape[1]
    line = iota((1, CORES * LANES), 1)
    piece_of = (line // (CAP * half)) % 2 * half + line % half
    inv = inverse[...]
    pieces = CAP * PIECES
    per_block = CORES * LANES // pieces
    source = iota((per_block, LANES), 0)
    lane = iota((per_block, LANES), 1)
    groups = groups_of(*rows)
    for b in range(0, len(groups), per_block):
        block = jnp.concatenate([part for part, _ in groups[b : b + per_block]], axis=0)
        whole = nt(stacked[...].reshape(PIECES * share, ROW), block)
        products = whole[:share]
        for n in range(1, PIECES):
            products = jnp.where(piece_of == n, whole[n * share : (n + 1) * share], products)
        best = []
        for c in range(CORES):
            total = products[:, c * LANES : (c + 1) * LANES]
            for shift in (1, 2, CAP * half):
                total = total + pltpu.roll(total, LANES - shift, 1)
            total = jnp.maximum(total, 0.0) * inv
            top = jnp.sum(total[:per_task], axis=0, keepdims=True)
            for n in range(1, share // per_task):
                top = jnp.maximum(
                    top, jnp.sum(total[n * per_task : (n + 1) * per_task], axis=0, keepdims=True)
                )
            best.append(top)
        table = jnp.where(source < per_block // CORES, best[0], best[1])
        scores = jnp.broadcast_to(counts[0:1, :], (per_block, counts.shape[1]))
        for n in range(CAP):
            at = lane == source % (per_block // CORES) * pieces + n * half
            column = jnp.sum(jnp.where(at, table, 0.0), axis=1, keepdims=True)
            scores = jnp.where(iota(scores.shape, 1) == first + n, column, scores)
        for n in range(per_block):
            for out, at in groups[b + n][1]:
                back[out][at] = scores[n : n + 1]


def finish_kernel(slots, strata_total, direct, picks, member, *refs):
    returned, out = refs[:-1], refs[-1]
    if direct:
        core = lax.axis_index("core")
        values = jnp.concatenate([ref[core] for ref in returned], axis=0)
    else:
        values = returned[0][:, 0, :]
    raw = jnp.max(values, axis=0, keepdims=True)
    counts = jnp.sum(values, axis=0, keepdims=True)
    held = iota(counts.shape, 1)
    held = jnp.logical_and(held >= slots, held < slots + strata_total)
    live = jnp.sum(jnp.where(held, counts, 0.0), axis=1, keepdims=True)
    weight = lax.rsqrt(strata_total * jnp.maximum(counts, 1.0))
    picked = jnp.sum(picks[...] * raw, axis=1, keepdims=True)
    picked = picked * jnp.sum(member[...] * weight, axis=1, keepdims=True) * jnp.sqrt(live)
    examples = picks.shape[0]
    square = iota((examples, LANES), 0) == iota((examples, LANES), 1)
    out[...] = jnp.sum(jnp.where(square, picked, 0.0), axis=0)[:examples]


def direct_order(owners):
    return [2, 1, 0, 3] if owners == 4 else [1, 0]


def direct_pairs(k, owners, columns):
    pairs = []
    for d in range(owners):
        for x in range(columns):
            for c in range(CORES):
                to = (d ^ k, x ^ (1 if k == 0 else c), c)
                pairs.append(
                    ((d * columns + x) * CORES + c, (to[0] * columns + to[1]) * CORES + to[2])
                )
    return pairs


def direct_return(mine, theirs, owners, columns, slots):
    def merge(a, b):
        return jnp.where(iota(a.shape, a.ndim - 1) < slots, jnp.maximum(a, b), a + b)

    chip = merge(mine, lax.ppermute(theirs, "core", SWAP))
    order = direct_order(owners)
    got = [
        lax.ppermute(chip[1 + k], ("dp", "x", "core"), direct_pairs(k, owners, columns)) for k in order
    ]
    far = functools.reduce(merge, [part for k, part in zip(order, got) if k > 0])
    return [chip[0], got[order.index(0)], far, lax.ppermute(far, "core", SWAP)]


def direct_rows(payload, owners, columns, norms):
    other = lax.ppermute(payload, "core", SWAP)
    arrived = []
    for k in direct_order(owners):
        rows = payload[0] if k == 0 else jnp.concatenate([payload[k], other[k]], axis=0)
        arrived.append(lax.ppermute(rows, ("dp", "x", "core"), direct_pairs(k, owners, columns)))
    arrived, norms = lax.optimization_barrier((arrived, norms))
    from_core = lax.ppermute(jnp.concatenate(arrived, axis=0), "core", SWAP)
    return [payload, other] + arrived + [from_core], norms


def shards(
    hidden,
    cotangent,
    adapter_down_weight,
    adapter_up_weight,
    width_projection_factor,
    rank_projection_factor,
    targets,
    strata,
    keep,
    shard_example_count,
    stratum_owner_table,
):
    examples = strata.shape[0]
    strata_total = stratum_owner_table.shape[0]
    owners, columns = lax.axis_size("dp"), lax.axis_size("x")
    slots = owners * CAP
    model, wide = width_projection_factor.shape
    rank, kr = rank_projection_factor.shape
    share = targets.shape[1]
    chips = owners * columns
    direct = columns == 2 and owners in (2, 4)

    def places(owner):
        if direct:
            return [jnp.bitwise_xor(lax.axis_index("dp"), owner)]
        return [owner * columns + n for n in range(columns)]

    lanes = -(-(slots + strata_total) // LANES) * LANES

    payload, dispatch, member = pl.pallas_call(
        functools.partial(project_kernel, places),
        out_shape=(
            jax.ShapeDtypeStruct((owners if direct else chips, CAP * PIECES, ROW), bf16),
            jax.ShapeDtypeStruct((examples, lanes), f32),
            jax.ShapeDtypeStruct((examples, lanes), f32),
        ),
        in_specs=[HBM] * 9,
        out_specs=(VMEM,) * 3,
        scratch_shapes=[
            pltpu.SMEM((examples,), i32),
            pltpu.SMEM((examples,), i32),
            pltpu.SMEM((strata_total,), i32),
            pltpu.SMEM((owners,), i32),
            pltpu.SMEM((slots + 1,), i32),
            pltpu.VMEM((2 * slots, SEQ, model), bf16),
            pltpu.VMEM((2 * rank, model), bf16),
            pltpu.VMEM((model, 2 * rank), bf16),
            pltpu.VMEM((model, wide), bf16),
            pltpu.VMEM((kr, rank), bf16),
            pltpu.VMEM((LANES, ROW), bf16),
            pltpu.SemaphoreType.DMA((3,)),
            pltpu.SemaphoreType.DMA((2 * slots,)),
            pltpu.SemaphoreType.DMA((7,)),
        ],
        compiler_params=pltpu.CompilerParams(vmem_limit_bytes=40 * 2**20),
        name="project",
    )(
        *in_hbm(
            strata,
            keep,
            stratum_owner_table,
            hidden.reshape(examples, SEQ, model),
            cotangent.reshape(examples, SEQ, model),
            adapter_down_weight.T,
            adapter_up_weight,
            width_projection_factor,
            rank_projection_factor.T,
        )
    )
    stacked, inverse, picks, counts = pl.pallas_call(
        functools.partial(norm_kernel, slots, direct),
        out_shape=(
            jax.ShapeDtypeStruct((PIECES, share, ROW), bf16),
            jax.ShapeDtypeStruct((share, LANES), f32),
            jax.ShapeDtypeStruct((examples, lanes), f32),
            jax.ShapeDtypeStruct((8, lanes), f32),
        ),
        in_specs=[
            pl.BlockSpec(memory_space=pltpu.SMEM), HBM, VMEM, VMEM, VMEM
        ],
        out_specs=(VMEM,) * 4,
        scratch_shapes=[pltpu.SemaphoreType.DMA((PIECES,))],
        compiler_params=pltpu.CompilerParams(vmem_limit_bytes=20 * 2**20),
        cost_estimate=pl.CostEstimate(flops=4 * share * FEAT, bytes_accessed=4 * share * FEAT, transcendentals=0),
        name="norms",
    )(shard_example_count, *in_hbm(targets), payload, dispatch, member)
    if direct:
        rows, (stacked, inverse, picks, counts) = direct_rows(payload, owners, columns, (stacked, inverse, picks, counts))
    else:
        mine = lax.all_to_all(payload, ("dp", "x"), split_axis=0, concat_axis=0, tiled=True)
        rows = [mine, lax.ppermute(mine, "core", SWAP)]
    places_back = [(owners + 1, CORES)] * 2 if direct else [(chips * CORES,)]
    back = pl.pallas_call(
        functools.partial(score_kernel, direct_groups if direct else gathered_groups, len(places_back)),
        out_shape=[jax.ShapeDtypeStruct((*place, 1, lanes), f32) for place in places_back],
        in_specs=[VMEM] * (3 + len(rows)),
        out_specs=[VMEM] * len(places_back),
        compiler_params=pltpu.CompilerParams(vmem_limit_bytes=40 * 2**20),
        name="score",
    )(stacked, inverse, counts, *rows)
    if direct:
        returned = direct_return(*back, owners, columns, slots)
    else:
        returned = [
            lax.all_to_all(back[0], ("dp", "x", "core"), split_axis=0, concat_axis=0, tiled=True)
        ]
    return pl.pallas_call(
        functools.partial(finish_kernel, slots, strata_total, direct),
        out_shape=jax.ShapeDtypeStruct((examples,), f32),
        in_specs=[VMEM] * (2 + len(returned)),
        out_specs=VMEM,
        compiler_params=pltpu.CompilerParams(vmem_limit_bytes=4 * 2**20),
        name="finish",
    )(picks, member, *returned)


def solution(mesh):
    sizes = [mesh.shape[name] for name in ("groups", "dp", "tgt")]
    fine = jax.sharding.Mesh(
        mesh.devices.reshape(sizes[0], sizes[1], sizes[2] // CORES, CORES),
        ("groups", "dp", "x", "core"),
    )
    every = P(("groups", "dp", "x", "core"))
    whole = P()
    return jax.shard_map(
        shards,
        mesh=fine,
        in_specs=(
            every, every, whole, whole, whole, whole,
            P(("groups", "dp"), ("x", "core"), None),
            every, every, every, whole,
        ),
        out_specs=every,
        check_vma=False,
    )
```

```python
import functools
import math

import jax
import jax.numpy as jnp
from jax import lax
from jax.experimental import pallas as pl
from jax.experimental.pallas import tpu as pltpu
from jax.sharding import PartitionSpec as P

FEAT = 8192
CAP = 2
TGT = 768
TASKS = 16
SEQ = 8
CORES = 2
SWAP = [(0, 1), (1, 0)]
LANES = 128
ROW = 1024
PIECES = FEAT // ROW
GROUP = 8
epsilon = 1e-06
bf16, f32, i32 = jnp.bfloat16, jnp.float32, jnp.int32

HBM = pl.BlockSpec(memory_space=pltpu.HBM)
VMEM = pl.BlockSpec(memory_space=pltpu.VMEM)


def nn(a, b):
    return jnp.dot(a, b, preferred_element_type=f32)


def nt(a, b):
    return lax.dot_general(a, b, (((1,), (1,)), ((), ())), preferred_element_type=f32)


def in_hbm(*arrays):
    return [pltpu.with_memory_space_constraint(a, pltpu.HBM) for a in arrays]


def iota(shape, dim):
    return lax.broadcasted_iota(i32, shape, dim)


def project_kernel(
    place_of, strata, keep, table, hidden, cotangent, down_t, up, width, rank_t,
    payload, dispatch, member,
    strata_s, keep_s, table_s, taken, chosen, x, adapters, adapters_t, width_v, rank_v, spread,
    small_sem, row_sem, weight_sem,
):
    examples, strata_total = strata_s.shape[0], table_s.shape[0]
    slots = x.shape[0] // 2
    owners = slots // CAP
    rank = down_t.shape[0]
    wide = width.shape[1]
    parts = 2
    early = 1
    depth = width.shape[0] // parts

    smalls = [
        pltpu.make_async_copy(a, b, small_sem.at[n])
        for n, (a, b) in enumerate(
            [(strata, strata_s), (keep, keep_s), (table, table_s)]
        )
    ]
    weights = [
        pltpu.make_async_copy(rank_t, rank_v, weight_sem.at[0]),
        pltpu.make_async_copy(down_t, adapters.at[pl.ds(0, rank)], weight_sem.at[1]),
        pltpu.make_async_copy(up, adapters.at[pl.ds(rank, rank)], weight_sem.at[2]),
    ] + [
        pltpu.make_async_copy(
            width.at[pl.ds(n * depth, depth)], width_v.at[pl.ds(n * depth, depth)], weight_sem.at[3 + n]
        )
        for n in range(parts)
    ]
    for copy in smalls + weights[: 3 + early]:
        copy.start()

    for n in range(owners):
        taken[n] = 0
    for n in range(slots + 1):
        chosen[n] = 0
    lane = iota((1, member.shape[1]), 1)
    for copy in smalls:
        copy.wait()
    for e in range(examples):
        stratum = strata_s[e]
        live = jnp.where(keep_s[e] == 1, 1, 0)
        owner = table_s[stratum]
        place = taken[owner]
        taken[owner] = place + live
        slot = jnp.where(jnp.logical_and(live == 1, place < CAP), owner * CAP + place, slots)
        chosen[slot] = e
        member[e : e + 1, :] = jnp.where(lane == slots + stratum, live.astype(f32), 0.0)
        dispatch[e : e + 1, :] = jnp.where(jnp.logical_and(lane == slot, lane < slots), 1.0, 0.0)
    rows = []
    for n in range(slots):
        rows.append(pltpu.make_async_copy(hidden.at[chosen[n]], x.at[n], row_sem.at[n]))
        rows.append(
            pltpu.make_async_copy(cotangent.at[chosen[n]], x.at[slots + n], row_sem.at[slots + n])
        )
    for copy in rows + weights[3 + early :]:
        copy.start()

    half = PIECES // 2
    kr = rank_v.shape[0]
    per_row = ROW // wide
    tokens = GROUP * SEQ
    lines = GROUP * half
    spread[...] = (iota((LANES, ROW), 1) // kr == iota((LANES, ROW), 0)).astype(f32).astype(bf16)
    weights[0].wait()
    up_line = iota((per_row * lines, kr), 0)
    pick_up = (per_row * (up_line % half) + up_line // lines == iota((per_row * lines, kr), 1))
    rank_up_rows = nn(pick_up.astype(f32).astype(bf16), rank_v[...]).astype(bf16)
    pick_down = iota((kr * lines, kr), 0) // lines == iota((kr * lines, kr), 1)
    rank_down_rows = nn(pick_down.astype(f32).astype(bf16), rank_v[...]).astype(bf16)
    up_at, up_token = iota((per_row * lines, tokens), 0), iota((per_row * lines, tokens), 1)
    up_mask = (up_at % lines) // half == up_token // SEQ
    down_at, down_token = iota((kr * lines, half * tokens), 0), iota((kr * lines, half * tokens), 1)
    down_mask = jnp.logical_and(
        (down_at % lines) // half == (down_token % tokens) // SEQ, down_at % half == down_token // tokens
    )
    rank_at = iota((lines, ROW), 1) % kr
    for copy in weights[1:3]:
        copy.wait()
    adapters_t[...] = adapters[...].T
    for copy in rows:
        copy.wait()

    for g in range(slots // GROUP):
        model = x.shape[2]
        def both(lo, size):
            return jnp.concatenate(
                [
                    x[g * GROUP : (g + 1) * GROUP, :, lo : lo + size].reshape(tokens, size),
                    x[slots + g * GROUP : slots + (g + 1) * GROUP, :, lo : lo + size].reshape(tokens, size),
                ],
                axis=0,
            )

        for n in range(parts):
            if g == 0:
                weights[3 + n].wait()
            span = pl.ds(n * depth, depth)
            lines_in = both(n * depth, depth)
            part = jnp.concatenate(
                [nn(lines_in, width_v[span, m : m + wide // 2]) for m in (0, wide // 2)], axis=1
            )
            projected = part if n == 0 else projected + part
            if n == 0:
                adapted = nn(both(0, model), adapters_t[...])
                down_act = adapted[:tokens, :rank].astype(bf16)
                up_back = adapted[tokens:, rank:].astype(bf16)
                left_up = jnp.where(up_mask, nt(rank_up_rows, down_act), 0.0).astype(bf16)
                left_down = nt(rank_down_rows, jnp.concatenate([up_back] * half, axis=0))
                left_down = jnp.where(down_mask, left_down, 0.0).astype(bf16)
        wide_hidden = projected[:tokens].astype(bf16)
        wide_back = projected[tokens:].astype(bf16)
        stacked = jnp.concatenate(
            [wide_hidden[:, n * LANES : (n + 1) * LANES] for n in range(half)], axis=0
        )
        down_grad = nn(left_down, stacked).astype(bf16)
        up_grad = nn(left_up, wide_back)
        up_rows = jnp.concatenate(
            [up_grad[n * lines : (n + 1) * lines] for n in range(per_row)], axis=1
        )
        repeated = nn(down_grad, spread[...])
        down_rows = repeated[:lines]
        for n in range(1, kr):
            down_rows = jnp.where(rank_at == n, repeated[n * lines : (n + 1) * lines], down_rows)

        per_owner = CAP * half
        for n in range(GROUP // CAP):
            owner = g * (GROUP // CAP) + n
            piece = jnp.concatenate(
                [
                    up_rows[n * per_owner : (n + 1) * per_owner],
                    down_rows[n * per_owner : (n + 1) * per_owner],
                ],
                axis=0,
            ).astype(bf16)
            for at in place_of(owner):
                payload[at] = piece


def norm_kernel(
    slots, direct, present, targets, payload, dispatch, member,
    stacked, inverse, picks, counts, sem,
):
    copies = [
        pltpu.make_async_copy(
            targets.at[0, :, pl.ds(n * ROW, ROW)], stacked.at[n], sem.at[n]
        )
        for n in range(PIECES)
    ]
    for copy in copies:
        copy.start()
    total = jnp.zeros((targets.shape[1], LANES), f32)
    for n in range(PIECES):
        copies[n].wait()
        for m in range(ROW // LANES):
            part = stacked[n, :, m * LANES : (m + 1) * LANES].astype(f32)
            total += part * part
    scale = math.sqrt(FEAT) / (TGT // TASKS)
    inverse[...] = jnp.broadcast_to(
        scale * lax.rsqrt(jnp.sum(total, axis=1, keepdims=True) + epsilon), inverse.shape
    )
    owners, pieces = slots // CAP, payload.shape[1]
    step = payload.shape[0] // owners
    values = jnp.concatenate([payload[n * step] for n in range(owners)], axis=0).astype(f32)
    squares = jnp.sum(values * values, axis=1, keepdims=True)
    at = (owners * pieces, picks.shape[1])
    line = iota(at, 0)
    owner = line // pieces
    if direct:
        owner = jnp.bitwise_xor(owner, lax.axis_index("dp"))
    slot = owner * CAP + line % pieces % (pieces // 2) // (PIECES // 2)
    squares = jnp.sum(jnp.where(slot == iota(at, 1), squares, 0.0), axis=0, keepdims=True)
    used = iota(picks.shape, 0) < present[0]
    picks[...] = jnp.where(used, dispatch[...] * lax.rsqrt(squares + epsilon), 0.0)
    held = jnp.sum(jnp.where(used, member[...], 0.0), axis=0, keepdims=True)
    counts[...] = jnp.broadcast_to(held, counts.shape)


def direct_groups(payload, other, *arrived):
    core = lax.axis_index("core")
    pieces = CAP * PIECES
    home = lambda n, on: [(0, (n, on)), (1, (n, on))]
    groups = [(payload[0], home(0, core)), (other[0], home(0, 1 - core))]
    arrived, from_core = arrived[:-1], arrived[-1]
    for out, on in ((0, core), (1, 1 - core)):
        start = 0
        for k, ref in zip(direct_order(lax.axis_size("dp")), arrived):
            span = ref.shape[0]
            rows = from_core[start : start + span] if out else ref[...]
            start += span
            if k == 0:
                groups.append((rows, home(1, on)))
            else:
                groups.append((rows[:pieces], [(out, (1 + k, on))]))
                groups.append((rows[pieces:], [(out, (1 + k, 1 - on))]))
    return groups


def gathered_groups(mine, other):
    core = lax.axis_index("core")
    sources = mine.shape[0]
    groups = []
    step = LANES // (CAP * PIECES)
    for b in range(0, sources, step):
        groups += [(mine[n], [(0, (n * CORES + core,))]) for n in range(b, b + step)]
        groups += [(other[n], [(0, (n * CORES + 1 - core,))]) for n in range(b, b + step)]
    return groups


def score_kernel(groups_of, outs, stacked, inverse, counts, *refs):
    rows, back = refs[:-outs], refs[-outs:]
    per_task = TGT // TASKS
    half = PIECES // 2
    first = lax.axis_index("dp") * CAP
    share = stacked.shape[1]
    line = iota((1, CORES * LANES), 1)
    piece_of = (line // (CAP * half)) % 2 * half + line % half
    inv = inverse[...]
    pieces = CAP * PIECES
    per_block = CORES * LANES // pieces
    source = iota((per_block, LANES), 0)
    lane = iota((per_block, LANES), 1)
    groups = groups_of(*rows)
    for b in range(0, len(groups), per_block):
        block = jnp.concatenate([part for part, _ in groups[b : b + per_block]], axis=0)
        whole = nt(stacked[...].reshape(PIECES * share, ROW), block)
        products = whole[:share]
        for n in range(1, PIECES):
            products = jnp.where(piece_of == n, whole[n * share : (n + 1) * share], products)
        best = []
        for c in range(CORES):
            total = products[:, c * LANES : (c + 1) * LANES]
            for shift in (1, 2, CAP * half):
                total = total + pltpu.roll(total, LANES - shift, 1)
            total = jnp.maximum(total, 0.0) * inv
            top = jnp.sum(total[:per_task], axis=0, keepdims=True)
            for n in range(1, share // per_task):
                top = jnp.maximum(
                    top, jnp.sum(total[n * per_task : (n + 1) * per_task], axis=0, keepdims=True)
                )
            best.append(top)
        table = jnp.where(source < per_block // CORES, best[0], best[1])
        scores = jnp.broadcast_to(counts[0:1, :], (per_block, counts.shape[1]))
        for n in range(CAP):
            at = lane == source % (per_block // CORES) * pieces + n * half
            column = jnp.sum(jnp.where(at, table, 0.0), axis=1, keepdims=True)
            scores = jnp.where(iota(scores.shape, 1) == first + n, column, scores)
        for n in range(per_block):
            for out, at in groups[b + n][1]:
                back[out][at] = scores[n : n + 1]


def finish_kernel(slots, strata_total, direct, picks, member, *refs):
    returned, out = refs[:-1], refs[-1]
    if direct:
        core = lax.axis_index("core")
        values = jnp.concatenate([ref[core] for ref in returned], axis=0)
    else:
        values = returned[0][:, 0, :]
    raw = jnp.max(values, axis=0, keepdims=True)
    counts = jnp.sum(values, axis=0, keepdims=True)
    held = iota(counts.shape, 1)
    held = jnp.logical_and(held >= slots, held < slots + strata_total)
    live = jnp.sum(jnp.where(held, counts, 0.0), axis=1, keepdims=True)
    weight = lax.rsqrt(strata_total * jnp.maximum(counts, 1.0))
    picked = jnp.sum(picks[...] * raw, axis=1, keepdims=True)
    picked = picked * jnp.sum(member[...] * weight, axis=1, keepdims=True) * jnp.sqrt(live)
    examples = picks.shape[0]
    square = iota((examples, LANES), 0) == iota((examples, LANES), 1)
    out[...] = jnp.sum(jnp.where(square, picked, 0.0), axis=0)[:examples]


def direct_order(owners):
    return [2, 1, 0, 3] if owners == 4 else [1, 0]


def direct_pairs(k, owners, columns):
    pairs = []
    for d in range(owners):
        for x in range(columns):
            for c in range(CORES):
                to = (d ^ k, x ^ (1 if k == 0 else c), c)
                pairs.append(
                    ((d * columns + x) * CORES + c, (to[0] * columns + to[1]) * CORES + to[2])
                )
    return pairs


def direct_return(mine, theirs, owners, columns, slots):
    def merge(a, b):
        return jnp.where(iota(a.shape, a.ndim - 1) < slots, jnp.maximum(a, b), a + b)

    chip = merge(mine, lax.ppermute(theirs, "core", SWAP))
    order = direct_order(owners)
    got = [
        lax.ppermute(chip[1 + k], ("dp", "x", "core"), direct_pairs(k, owners, columns)) for k in order
    ]
    far = functools.reduce(merge, [part for k, part in zip(order, got) if k > 0])
    return [chip[0], got[order.index(0)], far, lax.ppermute(far, "core", SWAP)]


def direct_rows(payload, owners, columns, norms):
    other = lax.ppermute(payload, "core", SWAP)
    arrived = []
    for k in direct_order(owners):
        rows = payload[0] if k == 0 else jnp.concatenate([payload[k], other[k]], axis=0)
        arrived.append(lax.ppermute(rows, ("dp", "x", "core"), direct_pairs(k, owners, columns)))
    arrived, norms = lax.optimization_barrier((arrived, norms))
    from_core = lax.ppermute(jnp.concatenate(arrived, axis=0), "core", SWAP)
    return [payload, other] + arrived + [from_core], norms


def shards(
    hidden,
    cotangent,
    adapter_down_weight,
    adapter_up_weight,
    width_projection_factor,
    rank_projection_factor,
    targets,
    strata,
    keep,
    shard_example_count,
    stratum_owner_table,
):
    examples = strata.shape[0]
    strata_total = stratum_owner_table.shape[0]
    owners, columns = lax.axis_size("dp"), lax.axis_size("x")
    slots = owners * CAP
    model, wide = width_projection_factor.shape
    rank, kr = rank_projection_factor.shape
    share = targets.shape[1]
    chips = owners * columns
    direct = columns == 2 and owners in (2, 4)

    def places(owner):
        if direct:
            return [jnp.bitwise_xor(lax.axis_index("dp"), owner)]
        return [owner * columns + n for n in range(columns)]

    lanes = -(-(slots + strata_total) // LANES) * LANES

    payload, dispatch, member = pl.pallas_call(
        functools.partial(project_kernel, places),
        out_shape=(
            jax.ShapeDtypeStruct((owners if direct else chips, CAP * PIECES, ROW), bf16),
            jax.ShapeDtypeStruct((examples, lanes), f32),
            jax.ShapeDtypeStruct((examples, lanes), f32),
        ),
        in_specs=[HBM] * 9,
        out_specs=(VMEM,) * 3,
        scratch_shapes=[
            pltpu.SMEM((examples,), i32),
            pltpu.SMEM((examples,), i32),
            pltpu.SMEM((strata_total,), i32),
            pltpu.SMEM((owners,), i32),
            pltpu.SMEM((slots + 1,), i32),
            pltpu.VMEM((2 * slots, SEQ, model), bf16),
            pltpu.VMEM((2 * rank, model), bf16),
            pltpu.VMEM((model, 2 * rank), bf16),
            pltpu.VMEM((model, wide), bf16),
            pltpu.VMEM((kr, rank), bf16),
            pltpu.VMEM((LANES, ROW), bf16),
            pltpu.SemaphoreType.DMA((3,)),
            pltpu.SemaphoreType.DMA((2 * slots,)),
            pltpu.SemaphoreType.DMA((7,)),
        ],
        compiler_params=pltpu.CompilerParams(vmem_limit_bytes=40 * 2**20),
        name="project",
    )(
        *in_hbm(
            strata,
            keep,
            stratum_owner_table,
            hidden.reshape(examples, SEQ, model),
            cotangent.reshape(examples, SEQ, model),
            adapter_down_weight.T,
            adapter_up_weight,
            width_projection_factor,
            rank_projection_factor.T,
        )
    )
    stacked, inverse, picks, counts = pl.pallas_call(
        functools.partial(norm_kernel, slots, direct),
        out_shape=(
            jax.ShapeDtypeStruct((PIECES, share, ROW), bf16),
            jax.ShapeDtypeStruct((share, LANES), f32),
            jax.ShapeDtypeStruct((examples, lanes), f32),
            jax.ShapeDtypeStruct((8, lanes), f32),
        ),
        in_specs=[
            pl.BlockSpec(memory_space=pltpu.SMEM), HBM, VMEM, VMEM, VMEM
        ],
        out_specs=(VMEM,) * 4,
        scratch_shapes=[pltpu.SemaphoreType.DMA((PIECES,))],
        compiler_params=pltpu.CompilerParams(vmem_limit_bytes=20 * 2**20),
        cost_estimate=pl.CostEstimate(flops=4 * share * FEAT, bytes_accessed=4 * share * FEAT, transcendentals=0),
        name="norms",
    )(shard_example_count, *in_hbm(targets), payload, dispatch, member)
    if direct:
        rows, (stacked, inverse, picks, counts) = direct_rows(payload, owners, columns, (stacked, inverse, picks, counts))
    else:
        mine = lax.all_to_all(payload, ("dp", "x"), split_axis=0, concat_axis=0, tiled=True)
        rows = [mine, lax.ppermute(mine, "core", SWAP)]
    places_back = [(owners + 1, CORES)] * 2 if direct else [(chips * CORES,)]
    back = pl.pallas_call(
        functools.partial(score_kernel, direct_groups if direct else gathered_groups, len(places_back)),
        out_shape=[jax.ShapeDtypeStruct((*place, 1, lanes), f32) for place in places_back],
        in_specs=[VMEM] * (3 + len(rows)),
        out_specs=[VMEM] * len(places_back),
        compiler_params=pltpu.CompilerParams(vmem_limit_bytes=40 * 2**20),
        name="score",
    )(stacked, inverse, counts, *rows)
    if direct:
        returned = direct_return(*back, owners, columns, slots)
    else:
        returned = [
            lax.all_to_all(back[0], ("dp", "x", "core"), split_axis=0, concat_axis=0, tiled=True)
        ]
    return pl.pallas_call(
        functools.partial(finish_kernel, slots, strata_total, direct),
        out_shape=jax.ShapeDtypeStruct((examples,), f32),
        in_specs=[VMEM] * (2 + len(returned)),
        out_specs=VMEM,
        compiler_params=pltpu.CompilerParams(vmem_limit_bytes=4 * 2**20),
        name="finish",
    )(picks, member, *returned)


def solution(mesh):
    sizes = [mesh.shape[name] for name in ("groups", "dp", "tgt")]
    fine = jax.sharding.Mesh(
        mesh.devices.reshape(sizes[0], sizes[1], sizes[2] // CORES, CORES),
        ("groups", "dp", "x", "core"),
    )
    every = P(("groups", "dp", "x", "core"))
    whole = P()
    return jax.shard_map(
        shards,
        mesh=fine,
        in_specs=(
            every, every, whole, whole, whole, whole,
            P(("groups", "dp"), ("x", "core"), None),
            every, every, every, whole,
        ),
        out_specs=every,
        check_vma=False,
    )
```

```python
import functools
import math

import jax
import jax.numpy as jnp
from jax import lax
from jax.experimental import pallas as pl
from jax.experimental.pallas import tpu as pltpu
from jax.sharding import PartitionSpec as P

FEAT = 8192
CAP = 2
TGT = 768
TASKS = 16
SEQ = 8
CORES = 2
SWAP = [(0, 1), (1, 0)]
LANES = 128
ROW = 1024
PIECES = FEAT // ROW
GROUP = 8
epsilon = 1e-06
bf16, f32, i32 = jnp.bfloat16, jnp.float32, jnp.int32

HBM = pl.BlockSpec(memory_space=pltpu.HBM)
VMEM = pl.BlockSpec(memory_space=pltpu.VMEM)


def nn(a, b):
    return jnp.dot(a, b, preferred_element_type=f32)


def nt(a, b):
    return lax.dot_general(a, b, (((1,), (1,)), ((), ())), preferred_element_type=f32)


def in_hbm(*arrays):
    return [pltpu.with_memory_space_constraint(a, pltpu.HBM) for a in arrays]


def iota(shape, dim):
    return lax.broadcasted_iota(i32, shape, dim)


def project_kernel(
    place_of, strata, keep, table, hidden, cotangent, down_t, up, width, rank_t,
    payload, dispatch, member,
    strata_s, keep_s, table_s, taken, chosen, x, adapters, adapters_t, width_v, rank_v, spread,
    small_sem, row_sem, weight_sem,
):
    examples, strata_total = strata_s.shape[0], table_s.shape[0]
    slots = x.shape[0] // 2
    owners = slots // CAP
    rank = down_t.shape[0]
    wide = width.shape[1]
    parts = 2
    early = 1
    depth = width.shape[0] // parts

    smalls = [
        pltpu.make_async_copy(a, b, small_sem.at[n])
        for n, (a, b) in enumerate(
            [(strata, strata_s), (keep, keep_s), (table, table_s)]
        )
    ]
    weights = [
        pltpu.make_async_copy(rank_t, rank_v, weight_sem.at[0]),
        pltpu.make_async_copy(down_t, adapters.at[pl.ds(0, rank)], weight_sem.at[1]),
        pltpu.make_async_copy(up, adapters.at[pl.ds(rank, rank)], weight_sem.at[2]),
    ] + [
        pltpu.make_async_copy(
            width.at[pl.ds(n * depth, depth)], width_v.at[pl.ds(n * depth, depth)], weight_sem.at[3 + n]
        )
        for n in range(parts)
    ]
    for copy in smalls + weights[: 3 + early]:
        copy.start()

    for n in range(owners):
        taken[n] = 0
    for n in range(slots + 1):
        chosen[n] = 0
    lane = iota((1, member.shape[1]), 1)
    for copy in smalls:
        copy.wait()
    for e in range(examples):
        stratum = strata_s[e]
        live = jnp.where(keep_s[e] == 1, 1, 0)
        owner = table_s[stratum]
        place = taken[owner]
        taken[owner] = place + live
        slot = jnp.where(jnp.logical_and(live == 1, place < CAP), owner * CAP + place, slots)
        chosen[slot] = e
        member[e : e + 1, :] = jnp.where(lane == slots + stratum, live.astype(f32), 0.0)
        dispatch[e : e + 1, :] = jnp.where(jnp.logical_and(lane == slot, lane < slots), 1.0, 0.0)
    rows = []
    for n in range(slots):
        rows.append(pltpu.make_async_copy(hidden.at[chosen[n]], x.at[n], row_sem.at[n]))
        rows.append(
            pltpu.make_async_copy(cotangent.at[chosen[n]], x.at[slots + n], row_sem.at[slots + n])
        )
    for copy in rows + weights[3 + early :]:
        copy.start()

    half = PIECES // 2
    kr = rank_v.shape[0]
    per_row = ROW // wide
    tokens = GROUP * SEQ
    lines = GROUP * half
    spread[...] = (iota((LANES, ROW), 1) // kr == iota((LANES, ROW), 0)).astype(f32).astype(bf16)
    weights[0].wait()
    up_line = iota((per_row * lines, kr), 0)
    pick_up = (per_row * (up_line % half) + up_line // lines == iota((per_row * lines, kr), 1))
    rank_up_rows = nn(pick_up.astype(f32).astype(bf16), rank_v[...]).astype(bf16)
    pick_down = iota((kr * lines, kr), 0) // lines == iota((kr * lines, kr), 1)
    rank_down_rows = nn(pick_down.astype(f32).astype(bf16), rank_v[...]).astype(bf16)
    up_at, up_token = iota((per_row * lines, tokens), 0), iota((per_row * lines, tokens), 1)
    up_mask = (up_at % lines) // half == up_token // SEQ
    down_at, down_token = iota((kr * lines, half * tokens), 0), iota((kr * lines, half * tokens), 1)
    down_mask = jnp.logical_and(
        (down_at % lines) // half == (down_token % tokens) // SEQ, down_at % half == down_token // tokens
    )
    rank_at = iota((lines, ROW), 1) % kr
    for copy in weights[1:3]:
        copy.wait()
    adapters_t[...] = adapters[...].T
    for copy in rows:
        copy.wait()

    for g in range(slots // GROUP):
        model = x.shape[2]
        def both(lo, size):
            return jnp.concatenate(
                [
                    x[g * GROUP : (g + 1) * GROUP, :, lo : lo + size].reshape(tokens, size),
                    x[slots + g * GROUP : slots + (g + 1) * GROUP, :, lo : lo + size].reshape(tokens, size),
                ],
                axis=0,
            )

        for n in range(parts):
            if g == 0:
                weights[3 + n].wait()
            span = pl.ds(n * depth, depth)
            lines_in = both(n * depth, depth)
            part = jnp.concatenate(
                [nn(lines_in, width_v[span, m : m + wide // 2]) for m in (0, wide // 2)], axis=1
            )
            projected = part if n == 0 else projected + part
            if n == 0:
                adapted = nn(both(0, model), adapters_t[...])
                down_act = adapted[:tokens, :rank].astype(bf16)
                up_back = adapted[tokens:, rank:].astype(bf16)
                left_up = jnp.where(up_mask, nt(rank_up_rows, down_act), 0.0).astype(bf16)
                left_down = nt(rank_down_rows, jnp.concatenate([up_back] * half, axis=0))
                left_down = jnp.where(down_mask, left_down, 0.0).astype(bf16)
        wide_hidden = projected[:tokens].astype(bf16)
        wide_back = projected[tokens:].astype(bf16)
        stacked = jnp.concatenate(
            [wide_hidden[:, n * LANES : (n + 1) * LANES] for n in range(half)], axis=0
        )
        down_grad = nn(left_down, stacked).astype(bf16)
        up_grad = nn(left_up, wide_back)
        up_rows = jnp.concatenate(
            [up_grad[n * lines : (n + 1) * lines] for n in range(per_row)], axis=1
        )
        repeated = nn(down_grad, spread[...])
        down_rows = repeated[:lines]
        for n in range(1, kr):
            down_rows = jnp.where(rank_at == n, repeated[n * lines : (n + 1) * lines], down_rows)

        per_owner = CAP * half
        for n in range(GROUP // CAP):
            owner = g * (GROUP // CAP) + n
            piece = jnp.concatenate(
                [
                    up_rows[n * per_owner : (n + 1) * per_owner],
                    down_rows[n * per_owner : (n + 1) * per_owner],
                ],
                axis=0,
            ).astype(bf16)
            for at in place_of(owner):
                payload[at] = piece


def norm_kernel(
    slots, direct, present, targets, payload, dispatch, member,
    stacked, inverse, picks, counts, sem,
):
    copies = [
        pltpu.make_async_copy(
            targets.at[0, :, pl.ds(n * ROW, ROW)], stacked.at[n], sem.at[n]
        )
        for n in range(PIECES)
    ]
    for copy in copies:
        copy.start()
    total = jnp.zeros((targets.shape[1], LANES), f32)
    for n in range(PIECES):
        copies[n].wait()
        for m in range(ROW // LANES):
            part = stacked[n, :, m * LANES : (m + 1) * LANES].astype(f32)
            total += part * part
    scale = math.sqrt(FEAT) / (TGT // TASKS)
    inverse[...] = jnp.broadcast_to(
        scale * lax.rsqrt(jnp.sum(total, axis=1, keepdims=True) + epsilon), inverse.shape
    )
    owners, pieces = slots // CAP, payload.shape[1]
    step = payload.shape[0] // owners
    values = jnp.concatenate([payload[n * step] for n in range(owners)], axis=0).astype(f32)
    squares = jnp.sum(values * values, axis=1, keepdims=True)
    at = (owners * pieces, picks.shape[1])
    line = iota(at, 0)
    owner = line // pieces
    if direct:
        owner = jnp.bitwise_xor(owner, lax.axis_index("dp"))
    slot = owner * CAP + line % pieces % (pieces // 2) // (PIECES // 2)
    squares = jnp.sum(jnp.where(slot == iota(at, 1), squares, 0.0), axis=0, keepdims=True)
    used = iota(picks.shape, 0) < present[0]
    picks[...] = jnp.where(used, dispatch[...] * lax.rsqrt(squares + epsilon), 0.0)
    held = jnp.sum(jnp.where(used, member[...], 0.0), axis=0, keepdims=True)
    counts[...] = jnp.broadcast_to(held, counts.shape)


def direct_groups(payload, other, *arrived):
    core = lax.axis_index("core")
    pieces = CAP * PIECES
    home = lambda n, on: [(0, (n, on)), (1, (n, on))]
    groups = [(payload[0], home(0, core)), (other[0], home(0, 1 - core))]
    arrived, from_core = arrived[:-1], arrived[-1]
    for out, on in ((0, core), (1, 1 - core)):
        start = 0
        for k, ref in zip(direct_order(lax.axis_size("dp")), arrived):
            span = ref.shape[0]
            rows = from_core[start : start + span] if out else ref[...]
            start += span
            if k == 0:
                groups.append((rows, home(1, on)))
            else:
                groups.append((rows[:pieces], [(out, (1 + k, on))]))
                groups.append((rows[pieces:], [(out, (1 + k, 1 - on))]))
    return groups


def gathered_groups(mine, other):
    core = lax.axis_index("core")
    sources = mine.shape[0]
    groups = []
    step = LANES // (CAP * PIECES)
    for b in range(0, sources, step):
        groups += [(mine[n], [(0, (n * CORES + core,))]) for n in range(b, b + step)]
        groups += [(other[n], [(0, (n * CORES + 1 - core,))]) for n in range(b, b + step)]
    return groups


def score_kernel(groups_of, outs, stacked, inverse, counts, *refs):
    rows, back = refs[:-outs], refs[-outs:]
    per_task = TGT // TASKS
    half = PIECES // 2
    first = lax.axis_index("dp") * CAP
    share = stacked.shape[1]
    line = iota((1, CORES * LANES), 1)
    piece_of = (line // (CAP * half)) % 2 * half + line % half
    inv = inverse[...]
    pieces = CAP * PIECES
    per_block = CORES * LANES // pieces
    source = iota((per_block, LANES), 0)
    lane = iota((per_block, LANES), 1)
    groups = groups_of(*rows)
    for b in range(0, len(groups), per_block):
        block = jnp.concatenate([part for part, _ in groups[b : b + per_block]], axis=0)
        whole = nt(stacked[...].reshape(PIECES * share, ROW), block)
        products = whole[:share]
        for n in range(1, PIECES):
            products = jnp.where(piece_of == n, whole[n * share : (n + 1) * share], products)
        best = []
        for c in range(CORES):
            total = products[:, c * LANES : (c + 1) * LANES]
            for shift in (1, 2, CAP * half):
                total = total + pltpu.roll(total, LANES - shift, 1)
            total = jnp.maximum(total, 0.0) * inv
            top = jnp.sum(total[:per_task], axis=0, keepdims=True)
            for n in range(1, share // per_task):
                top = jnp.maximum(
                    top, jnp.sum(total[n * per_task : (n + 1) * per_task], axis=0, keepdims=True)
                )
            best.append(top)
        table = jnp.where(source < per_block // CORES, best[0], best[1])
        scores = jnp.broadcast_to(counts[0:1, :], (per_block, counts.shape[1]))
        for n in range(CAP):
            at = lane == source % (per_block // CORES) * pieces + n * half
            column = jnp.sum(jnp.where(at, table, 0.0), axis=1, keepdims=True)
            scores = jnp.where(iota(scores.shape, 1) == first + n, column, scores)
        for n in range(per_block):
            for out, at in groups[b + n][1]:
                back[out][at] = scores[n : n + 1]


def finish_kernel(slots, strata_total, direct, picks, member, *refs):
    returned, out = refs[:-1], refs[-1]
    if direct:
        core = lax.axis_index("core")
        values = jnp.concatenate([ref[core] for ref in returned], axis=0)
    else:
        values = returned[0][:, 0, :]
    raw = jnp.max(values, axis=0, keepdims=True)
    counts = jnp.sum(values, axis=0, keepdims=True)
    held = iota(counts.shape, 1)
    held = jnp.logical_and(held >= slots, held < slots + strata_total)
    live = jnp.sum(jnp.where(held, counts, 0.0), axis=1, keepdims=True)
    weight = lax.rsqrt(strata_total * jnp.maximum(counts, 1.0))
    picked = jnp.sum(picks[...] * raw, axis=1, keepdims=True)
    picked = picked * jnp.sum(member[...] * weight, axis=1, keepdims=True) * jnp.sqrt(live)
    examples = picks.shape[0]
    square = iota((examples, LANES), 0) == iota((examples, LANES), 1)
    out[...] = jnp.sum(jnp.where(square, picked, 0.0), axis=0)[:examples]


def direct_order(owners):
    return [2, 1, 0, 3] if owners == 4 else [1, 0]


def direct_pairs(k, owners, columns):
    pairs = []
    for d in range(owners):
        for x in range(columns):
            for c in range(CORES):
                to = (d ^ k, x ^ (1 if k == 0 else c), c)
                pairs.append(
                    ((d * columns + x) * CORES + c, (to[0] * columns + to[1]) * CORES + to[2])
                )
    return pairs


def direct_return(mine, theirs, owners, columns, slots):
    def merge(a, b):
        return jnp.where(iota(a.shape, a.ndim - 1) < slots, jnp.maximum(a, b), a + b)

    chip = merge(mine, lax.ppermute(theirs, "core", SWAP))
    order = [2, 0, 1, 3] if owners == 4 else direct_order(owners)
    got = [
        lax.ppermute(chip[1 + k], ("dp", "x", "core"), direct_pairs(k, owners, columns)) for k in order
    ]
    far = functools.reduce(merge, [part for k, part in zip(order, got) if k > 0])
    return [chip[0], got[order.index(0)], far, lax.ppermute(far, "core", SWAP)]


def direct_rows(payload, owners, columns, norms):
    other = lax.ppermute(payload, "core", SWAP)
    arrived = []
    for k in direct_order(owners):
        rows = payload[0] if k == 0 else jnp.concatenate([payload[k], other[k]], axis=0)
        arrived.append(lax.ppermute(rows, ("dp", "x", "core"), direct_pairs(k, owners, columns)))
    arrived, norms = lax.optimization_barrier((arrived, norms))
    from_core = lax.ppermute(jnp.concatenate(arrived, axis=0), "core", SWAP)
    return [payload, other] + arrived + [from_core], norms


def shards(
    hidden,
    cotangent,
    adapter_down_weight,
    adapter_up_weight,
    width_projection_factor,
    rank_projection_factor,
    targets,
    strata,
    keep,
    shard_example_count,
    stratum_owner_table,
):
    examples = strata.shape[0]
    strata_total = stratum_owner_table.shape[0]
    owners, columns = lax.axis_size("dp"), lax.axis_size("x")
    slots = owners * CAP
    model, wide = width_projection_factor.shape
    rank, kr = rank_projection_factor.shape
    share = targets.shape[1]
    chips = owners * columns
    direct = columns == 2 and owners in (2, 4)

    def places(owner):
        if direct:
            return [jnp.bitwise_xor(lax.axis_index("dp"), owner)]
        return [owner * columns + n for n in range(columns)]

    lanes = -(-(slots + strata_total) // LANES) * LANES

    payload, dispatch, member = pl.pallas_call(
        functools.partial(project_kernel, places),
        out_shape=(
            jax.ShapeDtypeStruct((owners if direct else chips, CAP * PIECES, ROW), bf16),
            jax.ShapeDtypeStruct((examples, lanes), f32),
            jax.ShapeDtypeStruct((examples, lanes), f32),
        ),
        in_specs=[HBM] * 9,
        out_specs=(VMEM,) * 3,
        scratch_shapes=[
            pltpu.SMEM((examples,), i32),
            pltpu.SMEM((examples,), i32),
            pltpu.SMEM((strata_total,), i32),
            pltpu.SMEM((owners,), i32),
            pltpu.SMEM((slots + 1,), i32),
            pltpu.VMEM((2 * slots, SEQ, model), bf16),
            pltpu.VMEM((2 * rank, model), bf16),
            pltpu.VMEM((model, 2 * rank), bf16),
            pltpu.VMEM((model, wide), bf16),
            pltpu.VMEM((kr, rank), bf16),
            pltpu.VMEM((LANES, ROW), bf16),
            pltpu.SemaphoreType.DMA((3,)),
            pltpu.SemaphoreType.DMA((2 * slots,)),
            pltpu.SemaphoreType.DMA((7,)),
        ],
        compiler_params=pltpu.CompilerParams(vmem_limit_bytes=40 * 2**20),
        name="project",
    )(
        *in_hbm(
            strata,
            keep,
            stratum_owner_table,
            hidden.reshape(examples, SEQ, model),
            cotangent.reshape(examples, SEQ, model),
            adapter_down_weight.T,
            adapter_up_weight,
            width_projection_factor,
            rank_projection_factor.T,
        )
    )
    stacked, inverse, picks, counts = pl.pallas_call(
        functools.partial(norm_kernel, slots, direct),
        out_shape=(
            jax.ShapeDtypeStruct((PIECES, share, ROW), bf16),
            jax.ShapeDtypeStruct((share, LANES), f32),
            jax.ShapeDtypeStruct((examples, lanes), f32),
            jax.ShapeDtypeStruct((8, lanes), f32),
        ),
        in_specs=[
            pl.BlockSpec(memory_space=pltpu.SMEM), HBM, VMEM, VMEM, VMEM
        ],
        out_specs=(VMEM,) * 4,
        scratch_shapes=[pltpu.SemaphoreType.DMA((PIECES,))],
        compiler_params=pltpu.CompilerParams(vmem_limit_bytes=20 * 2**20),
        cost_estimate=pl.CostEstimate(flops=4 * share * FEAT, bytes_accessed=4 * share * FEAT, transcendentals=0),
        name="norms",
    )(shard_example_count, *in_hbm(targets), payload, dispatch, member)
    if direct:
        rows, (stacked, inverse, picks, counts) = direct_rows(payload, owners, columns, (stacked, inverse, picks, counts))
    else:
        mine = lax.all_to_all(payload, ("dp", "x"), split_axis=0, concat_axis=0, tiled=True)
        rows = [mine, lax.ppermute(mine, "core", SWAP)]
    places_back = [(owners + 1, CORES)] * 2 if direct else [(chips * CORES,)]
    back = pl.pallas_call(
        functools.partial(score_kernel, direct_groups if direct else gathered_groups, len(places_back)),
        out_shape=[jax.ShapeDtypeStruct((*place, 1, lanes), f32) for place in places_back],
        in_specs=[VMEM] * (3 + len(rows)),
        out_specs=[VMEM] * len(places_back),
        compiler_params=pltpu.CompilerParams(vmem_limit_bytes=40 * 2**20),
        name="score",
    )(stacked, inverse, counts, *rows)
    if direct:
        returned = direct_return(*back, owners, columns, slots)
    else:
        returned = [
            lax.all_to_all(back[0], ("dp", "x", "core"), split_axis=0, concat_axis=0, tiled=True)
        ]
    return pl.pallas_call(
        functools.partial(finish_kernel, slots, strata_total, direct),
        out_shape=jax.ShapeDtypeStruct((examples,), f32),
        in_specs=[VMEM] * (2 + len(returned)),
        out_specs=VMEM,
        compiler_params=pltpu.CompilerParams(vmem_limit_bytes=4 * 2**20),
        name="finish",
    )(picks, member, *returned)


def solution(mesh):
    sizes = [mesh.shape[name] for name in ("groups", "dp", "tgt")]
    fine = jax.sharding.Mesh(
        mesh.devices.reshape(sizes[0], sizes[1], sizes[2] // CORES, CORES),
        ("groups", "dp", "x", "core"),
    )
    every = P(("groups", "dp", "x", "core"))
    whole = P()
    return jax.shard_map(
        shards,
        mesh=fine,
        in_specs=(
            every, every, whole, whole, whole, whole,
            P(("groups", "dp"), ("x", "core"), None),
            every, every, every, whole,
        ),
        out_specs=every,
        check_vma=False,
    )
```
